256 devices in a mesh: space: 16 (over x_lo, z), mode: 16 (over y, x_hi, core).
Axes of the slice: x: 4 (x_hi: 2, x_lo: 2; x = x_hi * 2 + x_lo), y: 4, z: 8, core: 2. Of those that a mesh axis runs over, the one named last changes fastest.
Arguments:
- pressure: float32 [176, 176, 32, 128], P('mode', 'space'), may hold values from -6 to 6
- source: float32 [176, 176, 32, 128], P('mode', 'space'), may hold values from -6 to 6
- concentration: float32 [176, 176, 32, 128], P('mode', 'space'), may hold values from -6 to 6
- mean_cond: float32 [176, 32, 128], P('space'), may hold values from 1 to 10
- kl_cond: float32 [8, 176, 32, 128], P(None, 'space'), may hold values from -4 to 4
- mode_table: int32 [176, 8], replicated, may hold values from -1 to 3, as said below
Outputs:
- pressure_next: float32 [176, 176, 32, 128], P('mode', 'space')
- concentration_next: float32 [176, 176, 32, 128], P('mode', 'space')
The draws below stay inside these ranges and needn't reach their ends.
Inputs may be any that keep to these rules, and one draw needn't show every extreme that they name: `mode_table`: each row is either a multi-index of 8 degrees with total at most 3, or all -1; every such multi-index is exactly one row, in a shuffled order.
All inputs are finite; a program needn't handle non-finite values.
Results may differ from the reference program's by a relative error of at most 0.0036.
Values may be sent and summed in bfloat16 or wider, within the bound.
No kernel may reach another device: no remote copies, remote signals or barrier semaphores. Data moves between devices by JAX's collectives and lax.ppermute only.
A program may use at most 192 MiB of HBM per device.

```python
import math
import jax
import jax.numpy as jnp
import numpy as np
from jax import lax

P_SIZE = 176
KL = 8
ORDER = 3
CY = 32
CZ = 128
NX = 176


def draw_mode_table(key, part):
    key = jax.random.fold_in(key, 7)
    base = ORDER + 1
    counter = np.arange(base ** KL)
    powers = base ** np.arange(KL)
    lattice = counter[:, None] // powers[None, :] % base
    chosen = lattice[lattice.sum(axis=1) <= ORDER].astype(np.int32)
    filler = np.zeros((P_SIZE - chosen.shape[0], KL), dtype=np.int32) - 1
    mode_rows = np.concatenate([chosen, filler], axis=0)
    shuffle = jax.random.permutation(key, P_SIZE)
    return jnp.asarray(mode_rows)[shuffle]


def level_of(own_key, extent, cuts, least, largest):
    loudness = 1.0
    for dim, shards_of in cuts:
        heights = jax.random.uniform(jax.random.fold_in(jax.random.fold_in(own_key, 6), dim), (shards_of,), jnp.float32, least / len(cuts), largest / len(cuts))
        loudness = loudness * jnp.repeat(jnp.exp(heights), extent[dim] // shards_of).reshape((-1,) + (1,) * (len(extent) - 1 - dim))
    return loudness


def gaussian(key, shape, scale, bound, split=(), held_as=jnp.bfloat16):
    level = level_of(key, shape, split, -0.22, 0.18) if split else 1.0
    entries = jax.random.normal(key, shape, jnp.float32) * scale * level
    return jnp.minimum(jnp.maximum(entries, -bound), bound).astype(held_as)


def setup_inputs(seed: int = 0) -> dict:
    key_list = jax.random.split(jax.random.key(seed), 7)
    return {
        "pressure": gaussian(key_list[0], (P_SIZE, NX, CY, CZ), 1.0, 6.0, ((0, 16), (1, 16)), jnp.float32),
        "source": gaussian(key_list[1], (P_SIZE, NX, CY, CZ), 1.0, 6.0, ((0, 16), (1, 16)), jnp.float32),
        "concentration": gaussian(key_list[2], (P_SIZE, NX, CY, CZ), 1.0, 6.0, ((0, 16), (1, 16)), jnp.float32),
        "mean_cond": jnp.clip(jnp.exp(math.log(10.0) - 2.3025851 * jax.random.uniform(key_list[3], (NX, CY, CZ), jnp.float32) ** level_of(key_list[3], (NX, CY, CZ), ((0, 16),), -0.2, 0.2)), 1.0, 10.0),
        "kl_cond": gaussian(key_list[4], (KL, NX, CY, CZ), 1.0, 4.0, ((1, 16),), jnp.float32),
        "mode_table": draw_mode_table(jax.random.fold_in(key_list[6], 71), 0),
    }


OMEGA = 0.8
DISPERSION = 0.01
STEP = 0.05

def coupling(mode_table):
    is_valid = mode_table[:, 0] >= 0
    both_valid = is_valid[:, None] & is_valid[None, :]
    distance = jnp.abs(mode_table[:, None, :] - mode_table[None, :, :])
    total_gap = lax.optimization_barrier(jnp.sum(distance, axis=2))
    larger = jnp.maximum(mode_table[:, None, :], mode_table[None, :, :]).astype(jnp.float32)
    mean_part = jnp.where(both_valid & (total_gap == 0), 1.0, 0.0).astype(jnp.float32)
    kl_terms = jnp.where((both_valid & (total_gap == 1))[:, :, None] & (distance == 1), jnp.sqrt(jnp.maximum(larger, 1.0)), 0.0).astype(jnp.float32)
    tensor = jnp.concatenate([mean_part[:, None, :], jnp.transpose(kl_terms, (0, 2, 1))], axis=1)
    return tensor.astype(jnp.bfloat16)

def laplace(extended):
    centre = extended[:, 1:-1]
    padded = jnp.pad(centre, ((0, 0), (0, 0), (1, 1), (1, 1)))
    beside_all = extended[:, 2:] + extended[:, :-2]
    beside_all = beside_all + padded[:, :, 2:, 1:-1] + padded[:, :, :-2, 1:-1]
    beside_all = beside_all + padded[:, :, 1:-1, 2:] + padded[:, :, 1:-1, :-2]
    return 6.0 * centre - beside_all

def gradients(extended):
    centre = extended[:, 1:-1]
    padded = jnp.pad(centre, ((0, 0), (0, 0), (1, 1), (1, 1)))
    along_x = 0.5 * (extended[:, 2:] - extended[:, :-2])
    along_y = 0.5 * (padded[:, :, 2:, 1:-1] - padded[:, :, :-2, 1:-1])
    along_z = 0.5 * (padded[:, :, 1:-1, 2:] - padded[:, :, 1:-1, :-2])
    return (along_x, along_y, along_z)

def reference(pressure, source, concentration, mean_cond, kl_cond, mode_table):
    tensor = coupling(mode_table).astype(jnp.float32)
    flat_tensor = jnp.transpose(tensor.reshape(P_SIZE, (KL + 1) * P_SIZE))
    weights = jnp.concatenate([mean_cond[None], kl_cond], axis=0)
    weight_planes = jnp.moveaxis(weights, 1, 0)

    def contract(values):
        extended = jnp.pad(values, ((0, 0), (1, 1), (0, 0), (0, 0)))
        lap_field = lax.optimization_barrier(laplace(extended).astype(jnp.bfloat16))
        planes = jnp.moveaxis(lap_field, 1, 0)

        def one_plane(plane_items):
            plane_lap, weight = plane_items
            products = jnp.dot(flat_tensor, plane_lap.reshape(P_SIZE, -1).astype(jnp.float32), precision=lax.Precision.HIGHEST)
            products = products.reshape(KL + 1, P_SIZE, weight.shape[1], weight.shape[2])
            result = weight[0][None] * products[0]
            for kl_index in range(KL):
                result = result + weight[kl_index + 1][None] * products[kl_index + 1]
            return result
        summed = lax.map(one_plane, (planes, weight_planes))
        return jnp.moveaxis(summed, 0, 1)
    galerkin_press = contract(pressure)
    pressure_next = pressure + OMEGA * (source - galerkin_press) / (6.0 * mean_cond[None])
    galerkin_conc = contract(concentration)
    is_mean = (lax.optimization_barrier(jnp.sum(jnp.abs(mode_table), axis=1)) == 0).astype(jnp.int32)
    mean_row = jnp.argmax(is_mean).astype(jnp.int32)
    head_plane = lax.dynamic_slice_in_dim(pressure_next, mean_row, 1, 0)
    head_x, head_y, head_z = gradients(jnp.pad(head_plane, ((0, 0), (1, 1), (0, 0), (0, 0))))
    vel_x = -mean_cond[None] * head_x
    vel_y = -mean_cond[None] * head_y
    vel_z = -mean_cond[None] * head_z
    conc_x, conc_y, conc_z = gradients(jnp.pad(concentration, ((0, 0), (1, 1), (0, 0), (0, 0))))
    advection = vel_x * conc_x + vel_y * conc_y + vel_z * conc_z
    concentration_next = concentration - DISPERSION * galerkin_conc - STEP * advection
    return (pressure_next, concentration_next)
```

```python
import functools

import jax
import jax.numpy as jnp
from jax import lax
from jax.experimental import pallas as pl
from jax.experimental.pallas import tpu as pltpu
from jax.sharding import PartitionSpec as P

OMEGA = 0.8
DISPERSION = 0.01
STEP = 0.05

F32 = jnp.float32
BF16 = jnp.bfloat16

RANKS = 16
MODES = 11
PLANES = 11
CY = 32
CZ = 128
KL = 8
ALL = RANKS * MODES
HALVES = CY // RANKS
SPOTS = PLANES * HALVES
BODY = SPOTS * MODES
HIGH = BODY
LOW = BODY + SPOTS
ROWS_HEAD = 288
ROWS = 256
VMEM_LIMIT = 48 * 1024 * 1024


def vmem():
    return pl.BlockSpec(memory_space=pltpu.VMEM)


def smem():
    return pl.BlockSpec(memory_space=pltpu.SMEM)


def call(kernel, outs, ins, scratch, name, flops, moved):
    return pl.pallas_call(
        kernel,
        out_shape=outs,
        in_specs=ins,
        out_specs=jax.tree.map(lambda _: vmem(), outs),
        scratch_shapes=scratch,
        compiler_params=pltpu.CompilerParams(vmem_limit_bytes=VMEM_LIMIT),
        cost_estimate=pl.CostEstimate(flops=flops, bytes_accessed=moved, transcendentals=0),
        name=name,
    )


def coupling_kernel(column_ref, row_ref, out_ref):
    for block in range(ALL // 16):
        rows = pl.ds(block * 16, 16)
        columns = column_ref[rows, :]
        gap = jnp.zeros((16, 256), jnp.int32)
        steps = []
        for d in range(KL):
            column = columns[:, d : d + 1]
            row = row_ref[d : d + 1, :]
            step = jnp.abs(column - row)
            gap = gap + step
            steps.append((step, jnp.maximum(column, row)))
        valid = (columns[:, 0:1] >= 0) & (row_ref[0:1, :] >= 0)
        beside = valid & (gap == 1)
        for d in range(KL):
            step, larger = steps[d]
            root = jnp.sqrt(jnp.maximum(larger, 1).astype(F32))
            out_ref[d, rows, :] = jnp.where(beside & (step == 1), root, 0.0).astype(BF16)


def edge_masks():
    row = lax.broadcasted_iota(jnp.int32, (CY, CZ), 0)
    lane = lax.broadcasted_iota(jnp.int32, (CY, CZ), 1)
    return row == 0, row == CY - 1, lane == 0, lane == CZ - 1


def beside(tile, masks):
    first_row, last_row, first_lane, last_lane = masks
    y_less = jnp.where(first_row, 0.0, pltpu.roll(tile, 1, 0))
    y_more = jnp.where(last_row, 0.0, pltpu.roll(tile, CY - 1, 0))
    z_less = jnp.where(first_lane, 0.0, pltpu.roll(tile, 1, 1))
    z_more = jnp.where(last_lane, 0.0, pltpu.roll(tile, CZ - 1, 1))
    return y_less, y_more, z_less, z_more


def spread_rows(scratch, rows, row, tile):
    for half in range(HALVES):
        scratch[pl.ds(row + half * MODES, RANKS, stride=rows), :] = tile[half * RANKS : (half + 1) * RANKS]


def gather_rows(scratch, rows, row, gap):
    return jnp.concatenate(
        [scratch[pl.ds(row + half * gap, RANKS, stride=rows), :] for half in range(HALVES)], axis=0
    )


def pack(scratch, rows, out_ref):
    def one(rank, carry):
        for block in range(rows // 16):
            start = pl.multiple_of(rank * rows + block * 16, 16)
            out_ref[rank, pl.ds(block * 16, 16), :] = scratch[pl.ds(start, 16), :].astype(BF16)
        return carry

    lax.fori_loop(0, RANKS, one, 0)


def unpack(in_ref, rows, scratch):
    def one(rank, carry):
        for block in range(rows // 16):
            start = pl.multiple_of(rank * rows + block * 16, 16)
            scratch[pl.ds(start, 16), :] = in_ref[rank, pl.ds(block * 16, 16), :].astype(F32)
        return carry

    lax.fori_loop(0, RANKS, one, 0)


def laplace_rows(field_ref, low_ref, high_ref, offset, scratch, rows, finish):
    masks = edge_masks()

    def one_mode(m, carry):
        for x in range(PLANES):
            tile = field_ref[m, x]
            below = field_ref[m, x - 1] if x > 0 else low_ref[offset + m].astype(F32)
            above = field_ref[m, x + 1] if x < PLANES - 1 else high_ref[offset + m].astype(F32)
            y_less, y_more, z_less, z_more = beside(tile, masks)
            total = ((above + below) + (y_more + y_less)) + (z_more + z_less)
            image = (6.0 * tile - total).astype(BF16).astype(F32)
            for half in range(HALVES):
                scratch[pl.ds((x * HALVES + half) * MODES + m, RANKS, stride=rows), :] = image[
                    half * RANKS : (half + 1) * RANKS
                ]
            finish(m, x, tile, image)
        return carry

    lax.fori_loop(0, MODES, one_mode, 0)


def pressure_kernel(
    facts, field_ref, source_ref, low_ref, high_ref, mean_ref, send_ref, base_ref, scratch, scale
):
    rows = ROWS_HEAD
    scale[...] = OMEGA / (6.0 * mean_ref[...])

    def finish(m, x, tile, image):
        own = facts[4 + m].astype(F32)
        rest = source_ref[m, x] - own * (mean_ref[x] * image)
        base_ref[m, x] = tile + scale[x] * rest

    laplace_rows(field_ref, low_ref, high_ref, 0, scratch, rows, finish)
    slot = facts[2]
    for x in range(PLANES):
        head = field_ref[slot, x] + scale[x] * source_ref[slot, x]
        high = head.astype(BF16).astype(F32)
        for half in range(HALVES):
            part = slice(half * RANKS, (half + 1) * RANKS)
            scratch[pl.ds(HIGH + x * HALVES + half, RANKS, stride=rows), :] = high[part]
            scratch[pl.ds(LOW + x * HALVES + half, RANKS, stride=rows), :] = (head - high)[part]
    for rank in range(RANKS):
        start = rank * rows + LOW + SPOTS
        scratch[start : (rank + 1) * rows, :] = jnp.zeros((rows - LOW - SPOTS, CZ), F32)
    pack(scratch, rows, send_ref)


def concentration_kernel(
    facts, field_ref, low_ref, high_ref, mean_ref, send_ref, base_ref, scratch
):
    rows = ROWS

    def finish(m, x, tile, image):
        own = facts[4 + m].astype(F32) * DISPERSION
        base_ref[m, x] = tile - own * (mean_ref[x] * image)

    laplace_rows(field_ref, low_ref, high_ref, MODES, scratch, rows, finish)
    for rank in range(RANKS):
        scratch[rank * rows + BODY : (rank + 1) * rows, :] = jnp.zeros((rows - BODY, CZ), F32)
    pack(scratch, rows, send_ref)


def contract_kernel(with_head, facts, recv_ref, tensor_ref, kl_ref, mean_ref, send_ref, images, block, sums, outs):
    rows = ROWS_HEAD if with_head else ROWS
    unpack(recv_ref, rows, images)

    def one_plane(x, carry):
        for rank in range(RANKS):
            for half in range(HALVES):
                start = rank * rows + (x * HALVES + half) * MODES
                block[rank * 16 : (rank + 1) * 16, half * CZ : (half + 1) * CZ] = images[
                    pl.ds(start, 16), :
                ].astype(BF16)
        values = block[...]
        weights = kl_ref[x]
        total = jnp.zeros((ALL, HALVES * CZ), F32)
        for d in range(KL):
            product = jnp.dot(tensor_ref[d], values, preferred_element_type=F32)
            total = total + weights[d : d + 1] * product
        for half in range(HALVES):
            spot = x * HALVES + half
            sums[pl.ds(pl.multiple_of(spot * ALL, 8), ALL), :] = total[:, half * CZ : (half + 1) * CZ]
        for half in range(HALVES):
            spot = x * HALVES + half
            for rank in range(RANKS):
                outs[pl.ds(rank * rows + spot * MODES, 16), :] = sums[pl.ds(spot * ALL + rank * MODES, 16), :]
        return carry

    lax.fori_loop(0, PLANES, one_plane, 0)
    if with_head:
        owner, row, slot = facts[0], facts[1], facts[2]
        start = owner * rows
        known = images[pl.ds(start + HIGH, SPOTS), :] + images[pl.ds(start + LOW, SPOTS), :]
        image = images[pl.ds(start + slot, SPOTS, stride=MODES), :]
        total = sums[pl.ds(row, SPOTS, stride=ALL), :]
        mean = mean_ref[...]
        head = known - OMEGA * (mean * image + total) / (6.0 * mean)
        high = head.astype(BF16).astype(F32)
        for rank in range(RANKS):
            outs[rank * rows + HIGH : rank * rows + LOW, :] = high
            outs[rank * rows + LOW : rank * rows + LOW + SPOTS, :] = head - high
    pack(outs, rows, send_ref)


def pressure_result_kernel(recv_ref, base_ref, mean_ref, out_ref, head_ref, sums, scale):
    rows = ROWS_HEAD
    unpack(recv_ref, rows, sums)
    scale[...] = OMEGA / (6.0 * mean_ref[...])
    for x in range(PLANES):
        head_ref[x] = gather_rows(sums, rows, HIGH + x * HALVES, 1) + gather_rows(sums, rows, LOW + x * HALVES, 1)

    def one_mode(m, carry):
        for x in range(PLANES):
            total = gather_rows(sums, rows, x * HALVES * MODES + m, MODES)
            out_ref[m, x] = base_ref[m, x] - scale[x] * total
        return carry

    lax.fori_loop(0, MODES, one_mode, 0)


def advection_kernel(field_ref, low_ref, high_ref, base_ref, mean_ref, head_ref, head_low, head_high, out_ref, speed):
    masks = edge_masks()
    for x in range(PLANES):
        head = head_ref[x]
        below = head_ref[x - 1] if x > 0 else head_low[0]
        above = head_ref[x + 1] if x < PLANES - 1 else head_high[0]
        y_less, y_more, z_less, z_more = beside(head, masks)
        factor = (0.25 * STEP) * mean_ref[x]
        speed[0, x] = factor * (above - below)
        speed[1, x] = factor * (y_more - y_less)
        speed[2, x] = factor * (z_more - z_less)

    def one_mode(m, carry):
        for x in range(PLANES):
            tile = field_ref[m, x]
            below = field_ref[m, x - 1] if x > 0 else low_ref[MODES + m].astype(F32)
            above = field_ref[m, x + 1] if x < PLANES - 1 else high_ref[MODES + m].astype(F32)
            y_less, y_more, z_less, z_more = beside(tile, masks)
            moved = speed[0, x] * (above - below) + speed[1, x] * (y_more - y_less) + speed[2, x] * (z_more - z_less)
            out_ref[m, x] = base_ref[m, x] + moved
        return carry

    lax.fori_loop(0, MODES, one_mode, 0)


def concentration_result_kernel(recv_ref, base_ref, out_ref, sums):
    rows = ROWS
    unpack(recv_ref, rows, sums)

    def one_mode(m, carry):
        for x in range(PLANES):
            total = gather_rows(sums, rows, x * HALVES * MODES + m, MODES)
            out_ref[m, x] = base_ref[m, x] - DISPERSION * total
        return carry

    lax.fori_loop(0, MODES, one_mode, 0)


def local(pressure, source, concentration, mean_cond, kl_cond, mode_table):
    spaces = lax.axis_size("space")
    up = [(i, i + 1) for i in range(spaces - 1)]
    down = [(i + 1, i) for i in range(spaces - 1)]
    rank = lax.axis_index("mode")

    last = jnp.concatenate([pressure[:, -1], concentration[:, -1]], axis=0).astype(BF16)
    first = jnp.concatenate([pressure[:, 0], concentration[:, 0]], axis=0).astype(BF16)
    low = lax.ppermute(last, "space", up)
    high = lax.ppermute(first, "space", down)

    is_mean = jnp.sum(jnp.abs(mode_table), axis=1) == 0
    row = jnp.argmax(is_mean.astype(jnp.int32)).astype(jnp.int32)
    valid = lax.dynamic_slice_in_dim((mode_table[:, 0] >= 0).astype(jnp.int32), rank * MODES, MODES, 0)
    facts = jnp.concatenate(
        [jnp.stack([row // MODES, row, row % MODES, rank.astype(jnp.int32)]), valid, jnp.zeros((1,), jnp.int32)]
    )

    ordered = jnp.pad(
        mode_table.T.reshape(KL, RANKS, MODES), ((0, 0), (0, 0), (0, 16 - MODES)), constant_values=-1
    ).reshape(KL, RANKS * 16)
    tensor = call(
        coupling_kernel,
        jax.ShapeDtypeStruct((KL, ALL, 256), BF16),
        [vmem(), vmem()],
        [],
        "coupling",
        8 * ALL * 256 * 8,
        KL * ALL * 256 * 2,
    )(mode_table, ordered)

    own_kl = lax.dynamic_index_in_dim(kl_cond.reshape(KL, PLANES, HALVES, RANKS, CZ), rank, 3, keepdims=False)
    own_kl = jnp.swapaxes(own_kl.reshape(KL, PLANES, HALVES * CZ), 0, 1)
    own_mean = lax.dynamic_index_in_dim(mean_cond.reshape(SPOTS, RANKS, CZ), rank, 1, keepdims=False)

    field = jax.ShapeDtypeStruct(pressure.shape, F32)

    def message(rows):
        return jax.ShapeDtypeStruct((RANKS, rows, CZ), BF16)

    def exchange(rows_of):
        return lax.all_to_all(rows_of, "mode", 0, 0, tiled=True)

    size = pressure.size
    send_p, base_p = call(
        pressure_kernel,
        (message(ROWS_HEAD), field),
        [smem()] + [vmem()] * 5,
        [pltpu.VMEM((RANKS * ROWS_HEAD, CZ), F32), pltpu.VMEM((PLANES, CY, CZ), F32)],
        "pressure_images",
        size * 20,
        size * 14,
    )(facts, pressure, source, low, high, mean_cond)
    recv_p = exchange(send_p)
    send_c, base_c = call(
        concentration_kernel,
        (message(ROWS), field),
        [smem()] + [vmem()] * 4,
        [pltpu.VMEM((RANKS * ROWS, CZ), F32)],
        "concentration_images",
        size * 20,
        size * 10,
    )(facts, concentration, low, high, mean_cond)
    recv_c = exchange(send_c)

    def contract(with_head, received):
        rows = ROWS_HEAD if with_head else ROWS
        return call(
            functools.partial(contract_kernel, with_head),
            message(rows),
            [smem()] + [vmem()] * 4,
            [
                pltpu.VMEM((RANKS * rows + 16, CZ), F32),
                pltpu.VMEM((256, HALVES * CZ), BF16),
                pltpu.VMEM((SPOTS * ALL + 16, CZ), F32),
                pltpu.VMEM((RANKS * rows + 16, CZ), F32),
            ],
            "contract_pressure" if with_head else "contract_concentration",
            2 * KL * ALL * 256 * SPOTS * CZ,
            RANKS * rows * CZ * 4,
        )(facts, received, tensor, own_kl, own_mean)

    back_p = exchange(contract(True, recv_p))
    back_c = exchange(contract(False, recv_c))

    pressure_next, head = call(
        pressure_result_kernel,
        (field, jax.ShapeDtypeStruct(mean_cond.shape, F32)),
        [vmem()] * 3,
        [pltpu.VMEM((RANKS * ROWS_HEAD, CZ), F32), pltpu.VMEM((PLANES, CY, CZ), F32)],
        "pressure_result",
        size * 4,
        size * 10,
    )(back_p, base_p, mean_cond)
    head_low = lax.ppermute(head[-1:], "space", up)
    head_high = lax.ppermute(head[:1], "space", down)
    moved = call(
        advection_kernel,
        field,
        [vmem()] * 8,
        [pltpu.VMEM((3, PLANES, CY, CZ), F32)],
        "advection",
        size * 20,
        size * 12,
    )(concentration, low, high, base_c, mean_cond, head, head_low, head_high)
    concentration_next = call(
        concentration_result_kernel,
        field,
        [vmem()] * 2,
        [pltpu.VMEM((RANKS * ROWS, CZ), F32)],
        "concentration_result",
        size * 4,
        size * 10,
    )(back_c, moved)
    return (pressure_next, concentration_next)


def solution(mesh):
    return jax.shard_map(
        local,
        mesh=mesh,
        in_specs=(
            P("mode", "space", None, None),
            P("mode", "space", None, None),
            P("mode", "space", None, None),
            P("space", None, None),
            P(None, "space", None, None),
            P(),
        ),
        out_specs=(P("mode", "space", None, None), P("mode", "space", None, None)),
        check_vma=False,
    )
```

```python
import functools
import itertools

import jax
import jax.numpy as jnp
import numpy as np
from jax import lax
from jax.experimental import pallas as pl
from jax.experimental.pallas import tpu as pltpu
from jax.sharding import PartitionSpec as P

OMEGA = 0.8
DISPERSION = 0.01
STEP = 0.05
ORDER = 3

F32 = jnp.float32
BF16 = jnp.bfloat16

RANKS = 16
MODES = 11
PLANES = 11
CY = 32
CZ = 128
KL = 8
ALL = RANKS * MODES
SLAB = PLANES * CY
SHARE = SLAB // RANKS
FULL = 24
BODY = SHARE * MODES
PAD = 8
SPACED = SLAB + PAD

SENT_HIGH = 2 * BODY
SENT_LOW = SENT_HIGH + SHARE
SENT = SENT_LOW + SHARE
HIGH = BODY
LOW = BODY + SHARE
ROWS_HEAD = 288
ROWS = 256
STRIDE = SENT + PAD

EDGE_RANKS = (0, 1, RANKS - 2, RANKS - 1)
LIMIT = 60 * 1024 * 1024

INDICES = sorted(
    (t for t in itertools.product(range(ORDER + 1), repeat=KL) if sum(t) <= ORDER), key=lambda t: (sum(t), t)
)
PLACE = {t: i for i, t in enumerate(INDICES)}
NEIGHBOURS = [
    [
        (d, max(t[d], t[d] + step), PLACE[t[:d] + (t[d] + step,) + t[d + 1 :]])
        for d in range(KL)
        for step in (-1, 1)
        if t[:d] + (t[d] + step,) + t[d + 1 :] in PLACE
    ]
    for t in INDICES
]
VALID = len(INDICES)
POWERS = (ORDER + 1) ** np.arange(KL)
CODES = (np.array(INDICES) * POWERS).sum(axis=1).astype(np.int32)
OWNER = VALID


def vmem():
    return pl.BlockSpec(memory_space=pltpu.VMEM)


def smem():
    return pl.BlockSpec(memory_space=pltpu.SMEM)


def hbm():
    return pl.BlockSpec(memory_space=pltpu.HBM)


def call(kernel, outs, ins, scratch, name, flops, moved, aliases=None):
    return pl.pallas_call(
        kernel,
        out_shape=outs,
        in_specs=ins,
        out_specs=jax.tree.map(lambda _: hbm(), outs),
        scratch_shapes=scratch,
        input_output_aliases=aliases or {},
        compiler_params=pltpu.CompilerParams(vmem_limit_bytes=LIMIT),
        cost_estimate=pl.CostEstimate(flops=flops, bytes_accessed=moved, transcendentals=0),
        name=name,
    )


def start_all(sems, pairs):
    copies = [pltpu.make_async_copy(source, target, sems.at[i]) for i, (source, target) in enumerate(pairs)]
    for copy in copies:
        copy.start()
    return copies


def loop(first, last, work):
    def one(i, carry):
        work(i)
        return carry

    lax.fori_loop(first, last, one, 0)


def edge_masks():
    row = lax.broadcasted_iota(jnp.int32, (CY, CZ), 0)
    lane = lax.broadcasted_iota(jnp.int32, (CY, CZ), 1)
    return row == 0, row == CY - 1, lane == 0, lane == CZ - 1


def rows_of(ref, start):
    return ref[pl.ds(start, CY), :]


def beside(ref, start, tile, masks):
    first_row, last_row, first_lane, last_lane = masks
    y_less = jnp.where(first_row, 0.0, rows_of(ref, start - 1))
    y_more = jnp.where(last_row, 0.0, rows_of(ref, start + 1))
    z_less = jnp.where(first_lane, 0.0, pltpu.roll(tile, 1, 1))
    z_more = jnp.where(last_lane, 0.0, pltpu.roll(tile, CZ - 1, 1))
    return y_less, y_more, z_less, z_more


def laplace(ref, base, x, masks, outer=None):
    start = base + x * CY
    tile = rows_of(ref, start)
    y_less, y_more, z_less, z_more = beside(ref, start, tile, masks)
    total = (y_more + y_less) + (z_more + z_less)
    if x > 0:
        total = total + rows_of(ref, start - CY)
    if x < PLANES - 1:
        total = total + rows_of(ref, start + CY)
    if outer is not None:
        total = total + outer
    return tile, 6.0 * tile - total


def rounded(tile):
    return tile.astype(BF16).astype(F32)


def copy_share(target, to, source, start):
    for part in range(0, FULL, 8):
        target[pl.ds(to + part, 8), :] = source[pl.ds(start + part, 8), :]


def pack_rank(scratch, start, out_ref, slot, blocks):
    for block in range(blocks):
        out_ref[slot, pl.ds(block * 16, 16), :] = scratch[pl.ds(start + block * 16, 16), :].astype(BF16)


def unpack_rank(in_ref, rank, scratch, stride, blocks):
    for block in blocks:
        start = pl.multiple_of(rank * stride + block * 16, 8)
        scratch[pl.ds(start, 16), :] = in_ref[rank, pl.ds(block * 16, 16), :].astype(F32)


def inner_kernel(
    table_ref, mean_hbm, pressure_hbm, source_hbm, concentration_hbm, send_hbm, part_hbm,
    fields, source, mean, image, high, low, scratch, strip, sems, extra_sems, send_sems, part_sems,
):
    inputs = (pressure_hbm, concentration_hbm)

    def base_of(index, m):
        return pl.multiple_of(PAD + (index * MODES + m) * SPACED, 8)

    def fetch(index, m):
        target = fields.at[pl.ds(base_of(index, m), SLAB), :]
        return pltpu.make_async_copy(inputs[index].at[m], target, sems.at[index, m])

    for index in range(2):
        for m in range(MODES):
            fetch(index, m).start()
    total = jnp.sum(jnp.abs(table_ref[...]).astype(F32), axis=0, keepdims=True)
    place = lax.broadcasted_iota(jnp.int32, (1, ALL), 1).astype(F32)
    row = jnp.min(jnp.where(total == 0.0, place, float(ALL))).astype(jnp.int32)
    slot = lax.rem(row, MODES)
    extra = start_all(extra_sems, [(source_hbm.at[slot], source), (mean_hbm, mean)])
    masks = edge_masks()

    for index in range(2):

        def one_mode(m):
            fetch(index, m).wait()
            for x in range(PLANES):
                image[pl.ds(x * CY, CY), :] = laplace(fields, base_of(index, m), x, masks)[1]
            for rank in range(RANKS):
                copy_share(scratch, rank * STRIDE + (index * MODES + m) * SHARE, image, rank * SHARE)

        loop(0, MODES, one_mode)
    for copy in extra:
        copy.wait()
    for x in range(PLANES):
        rows = pl.ds(x * CY, CY)
        head = rows_of(fields, base_of(0, slot) + x * CY) + (OMEGA / (6.0 * mean[rows, :])) * source[rows, :]
        top = rounded(head)
        high[rows, :] = top
        low[rows, :] = head - top
    for rank in range(RANKS):
        copy_share(scratch, rank * STRIDE + SENT_HIGH, high, rank * SHARE)
        copy_share(scratch, rank * STRIDE + SENT_LOW, low, rank * SHARE)
    parts = start_all(
        part_sems,
        [(scratch.at[pl.ds(rank * STRIDE, SENT), :], part_hbm.at[i]) for i, rank in enumerate(EDGE_RANKS)],
    )

    def send(rank):
        return pltpu.make_async_copy(strip.at[rank], send_hbm.at[rank], send_sems.at[rank])

    def go(rank):
        pack_rank(scratch, pl.multiple_of(rank * STRIDE, 8), strip, rank, SENT // 16)
        send(rank).start()

    loop(2, RANKS - 2, go)
    for copy in parts:
        copy.wait()
    loop(2, RANKS - 2, lambda rank: send(rank).wait())


def outer_kernel(part_hbm, low_hbm, high_hbm, send_in, send_hbm, part, low, high, halo, strip, sems, send_sems):
    parts = [(part_hbm.at[i], part.at[pl.ds(i * STRIDE, SENT), :]) for i in range(4)]
    for copy in start_all(sems, parts + [(low_hbm, low), (high_hbm, high)]):
        copy.wait()

    def spread(mode):
        halo[pl.ds(0, CY), :] = low[mode].astype(F32)
        halo[pl.ds(CY, CY), :] = high[mode].astype(F32)
        row = mode * SHARE
        for i, at, of, count in (
            (0, 0, 0, SHARE),
            (1, 0, SHARE, CY - SHARE),
            (2, 2 * SHARE - CY, CY, CY - SHARE),
            (3, 0, 2 * CY - SHARE, SHARE),
        ):
            rows = pl.ds(i * STRIDE + row + at, count)
            part[rows, :] = part[rows, :] - halo[pl.ds(of, count), :]

    loop(0, 2 * MODES, spread)
    sends = []
    for i, rank in enumerate(EDGE_RANKS):
        pack_rank(part, i * STRIDE, strip, i, SENT // 16)
        send = pltpu.make_async_copy(strip.at[i], send_hbm.at[rank], send_sems.at[i])
        send.start()
        sends.append(send)
    for send in sends:
        send.wait()


def base_kernel(
    rank_ref, table_ref, pressure_hbm, source_hbm, concentration_hbm, mean_hbm, low_hbm, high_hbm,
    base_p_hbm, base_c_hbm,
    fields, source, mean, low, high, base_p, base_c, scale, sems, out_sems,
):
    copies = start_all(
        sems,
        [(mean_hbm, mean), (low_hbm, low), (high_hbm, high)]
        + [(pressure_hbm.at[m], fields.at[pl.ds(PAD + m * SPACED, SLAB), :]) for m in range(MODES)]
        + [(concentration_hbm.at[m], fields.at[pl.ds(PAD + (MODES + m) * SPACED, SLAB), :]) for m in range(MODES)]
        + [(source_hbm, source)],
    )
    for copy in copies:
        copy.wait()
    scale[...] = OMEGA / (6.0 * mean[...])
    masks = edge_masks()

    def one_mode(m):
        own = (table_ref[0, rank_ref[0] * MODES + m] >= 0).astype(F32)
        for index in range(2):
            base = pl.multiple_of(PAD + (index * MODES + m) * SPACED, 8)
            for x in range(PLANES):
                outer = None
                if x == 0:
                    outer = low[index * MODES + m].astype(F32)
                elif x == PLANES - 1:
                    outer = high[index * MODES + m].astype(F32)
                tile, image = laplace(fields, base, x, masks, outer)
                rows = pl.ds(x * CY, CY)
                term = own * (mean[rows, :] * rounded(image))
                if index == 0:
                    base_p[m, rows, :] = tile + scale[rows, :] * (source[m, rows, :] - term)
                else:
                    base_c[m, rows, :] = tile - DISPERSION * term

    loop(0, MODES, one_mode)
    for copy in start_all(out_sems, [(base_p, base_p_hbm), (base_c, base_c_hbm)]):
        copy.wait()


def contract_kernel(
    index, places, recv_hbm, kl_hbm, mean_hbm, send_hbm,
    recv, kl, mean, images, ordered, weights, outs, strip, recv_sems, sems, send_sems,
):
    rows = ROWS_HEAD if index == 0 else ROWS
    spans = ((0, 16), (30, 33)) if index == 0 else ((15, 31),)
    blocks = [block for first, last in spans for block in range(first, last)]

    def fetch(rank, part):
        first, last = spans[part]
        span = pl.ds(first * 16, (last - first) * 16)
        return pltpu.make_async_copy(recv_hbm.at[rank, span, :], recv.at[rank, span, :], recv_sems.at[part, rank])

    def begin(rank):
        for part in range(len(spans)):
            fetch(rank, part).start()

    loop(0, RANKS, begin)
    others = start_all(sems, [(kl_hbm, kl), (mean_hbm, mean)])

    def clear(rank):
        start = pl.multiple_of(rank * STRIDE, 8)
        outs[pl.ds(start, rows), :] = jnp.zeros((rows, CZ), F32)

    loop(0, RANKS, clear)
    for copy in others:
        copy.wait()
    for larger in range(ORDER):
        root = float(np.sqrt(np.float32(larger + 1)).astype(jnp.bfloat16))
        for d in range(KL):
            weights[larger * KL + d] = root * kl[d]

    def spread(rank):
        for part in range(len(spans)):
            fetch(rank, part).wait()
        unpack_rank(recv, rank, images, STRIDE, blocks)

    loop(0, RANKS, spread)
    for i in range(VALID):
        copy_share(ordered, i * FULL, images, places[i] + index * BODY)
    for part in range(0, FULL, 8):
        count = min(8, SHARE - part)
        held = [weights[i, pl.ds(part, 8), :] for i in range(ORDER * KL)]
        for i in range(VALID):
            total = None
            for d, larger, other in NEIGHBOURS[i]:
                term = held[(larger - 1) * KL + d] * ordered[pl.ds(other * FULL + part, 8), :]
                total = term if total is None else total + term
            outs[pl.ds(places[i] + part, count), :] = total[:count]
    if index == 0:
        start = places[OWNER]
        known = images[pl.ds(start + SENT_HIGH, SHARE), :] + images[pl.ds(start + SENT_LOW, SHARE), :]
        image = ordered[pl.ds(0, SHARE), :]
        total = outs[pl.ds(places[0], SHARE), :]
        here = mean[pl.ds(0, SHARE), :]
        head = known - OMEGA * (here * image + total) / (6.0 * here)
        top = rounded(head)
        for rank in range(RANKS):
            outs[pl.ds(rank * STRIDE + HIGH, SHARE), :] = top
            outs[pl.ds(rank * STRIDE + LOW, SHARE), :] = head - top

    def send(rank):
        return pltpu.make_async_copy(strip.at[rank], send_hbm.at[rank], send_sems.at[rank])

    def go(rank):
        pack_rank(outs, pl.multiple_of(rank * STRIDE, 8), strip, rank, rows // 16)
        send(rank).start()

    loop(0, RANKS, go)
    loop(0, RANKS, lambda rank: send(rank).wait())


def result_kernel(index, recv_hbm, base_hbm, mean_hbm, out_hbm, *rest):
    rows = ROWS if index else ROWS_HEAD
    stride = rows + PAD
    head_hbm = None if index else rest[0]
    recv, base, mean, scale, sums, head, out, recv_sems, base_sems, sems, extra_sems = rest[0 if index else 1 :]

    def fetch(rank):
        return pltpu.make_async_copy(recv_hbm.at[rank], recv.at[rank], recv_sems.at[rank])

    def fetch_base(m):
        target = base.at[pl.ds(pl.multiple_of(m * SPACED, 8), SLAB), :]
        return pltpu.make_async_copy(base_hbm.at[m], target, base_sems.at[m])

    def leave(m):
        source = out.at[pl.ds(pl.multiple_of(m * SPACED, 8), SLAB), :]
        return pltpu.make_async_copy(source, out_hbm.at[m], sems.at[m])

    loop(0, RANKS, lambda rank: fetch(rank).start())
    loop(0, MODES, lambda m: fetch_base(m).start())
    if index == 0:
        fetch_mean = pltpu.make_async_copy(mean_hbm, mean, extra_sems.at[0])
        fetch_mean.start()

    def spread(rank):
        fetch(rank).wait()
        unpack_rank(recv, rank, sums, stride, range(rows // 16))

    loop(0, RANKS, spread)
    if index == 0:
        fetch_mean.wait()
        scale[pl.ds(0, SLAB), :] = OMEGA / (6.0 * mean[...])
        for rank in range(RANKS):
            for part in range(0, FULL, 8):
                at = rank * stride + part
                head[pl.ds(rank * SHARE + part, 8), :] = sums[pl.ds(at + HIGH, 8), :] + sums[pl.ds(at + LOW, 8), :]
        head_out = pltpu.make_async_copy(head.at[pl.ds(0, SLAB), :], head_hbm, extra_sems.at[1])
        head_out.start()

    def one_mode(m):
        fetch_base(m).wait()
        for rank in range(RANKS):
            for part in range(0, FULL, 8):
                at = pl.ds(m * SPACED + rank * SHARE + part, 8)
                factor = DISPERSION if index else scale[pl.ds(rank * SHARE + part, 8), :]
                out[at, :] = base[at, :] - factor * sums[pl.ds(rank * stride + m * SHARE + part, 8), :]
        leave(m).start()

    loop(0, MODES, one_mode)
    if index == 0:
        head_out.wait()
    loop(0, MODES, lambda m: leave(m).wait())


def advection_kernel(
    field_hbm, low_hbm, high_hbm, base_hbm, mean_hbm, head_hbm, head_low_hbm, head_high_hbm, out_hbm,
    field, low, high, base, mean, head, head_low, head_high, out, speed, sems, out_sems,
):
    copies = start_all(
        sems,
        [
            (head_hbm, head.at[pl.ds(PAD, SLAB), :]),
            (head_low_hbm, head_low),
            (head_high_hbm, head_high),
            (mean_hbm, mean),
            (low_hbm, low),
            (high_hbm, high),
            (base_hbm, base),
        ]
        + [(field_hbm.at[m], field.at[pl.ds(PAD + m * SLAB, SLAB), :]) for m in range(MODES)],
    )
    masks = edge_masks()

    def steps(ref, base, x, outer):
        start = base + x * CY
        below = rows_of(ref, start - CY) if x > 0 else outer(0)
        above = rows_of(ref, start + CY) if x < PLANES - 1 else outer(1)
        y_less, y_more, z_less, z_more = beside(ref, start, rows_of(ref, start), masks)
        return above - below, y_more - y_less, z_more - z_less

    for copy in copies[:4]:
        copy.wait()
    for x in range(PLANES):
        rows = pl.ds(x * CY, CY)
        factor = (0.25 * STEP) * mean[rows, :]
        for axis, step in enumerate(steps(head, PAD, x, lambda side: (head_low, head_high)[side][...])):
            speed[axis, rows, :] = factor * step
    for copy in copies[4:]:
        copy.wait()

    def leave(m):
        return pltpu.make_async_copy(out.at[m], out_hbm.at[m], out_sems.at[m])

    def one_mode(m):
        for x in range(PLANES):
            rows = pl.ds(x * CY, CY)
            along = steps(
                field, pl.multiple_of(PAD + m * SLAB, 8), x, lambda side: (low, high)[side][MODES + m].astype(F32)
            )
            moved = sum(speed[axis, rows, :] * step for axis, step in enumerate(along))
            out[m, rows, :] = base[m, rows, :] + moved
        leave(m).start()

    loop(0, MODES, one_mode)
    loop(0, MODES, lambda m: leave(m).wait())


def local(pressure, source, concentration, mean_cond, kl_cond, mode_table):
    shape = pressure.shape
    spaces = lax.axis_size("space")
    up = [(i, i + 1) for i in range(spaces - 1)]
    down = [(i + 1, i) for i in range(spaces - 1)]
    rank = lax.axis_index("mode").astype(jnp.int32)
    table = mode_table.T
    size = pressure.size
    last = jnp.concatenate([pressure[:, -1], concentration[:, -1]], axis=0).astype(BF16)
    first = jnp.concatenate([pressure[:, 0], concentration[:, 0]], axis=0).astype(BF16)
    low = lax.ppermute(last, "space", up)
    high = lax.ppermute(first, "space", down)

    pressure, source, concentration = (a.reshape(MODES, SLAB, CZ) for a in (pressure, source, concentration))
    mean_cond = mean_cond.reshape(SLAB, CZ)
    kl_cond = kl_cond.reshape(KL, SLAB, CZ)

    field = jax.ShapeDtypeStruct(pressure.shape, F32)
    plane = jax.ShapeDtypeStruct(mean_cond.shape, F32)
    dma = pltpu.SemaphoreType.DMA
    field_vmem = pltpu.VMEM(pressure.shape, F32)
    halo_vmem = pltpu.VMEM((2 * MODES, CY, CZ), BF16)
    edge_vmem = pltpu.VMEM((CY, CZ), F32)

    def rows_vmem(rows):
        return pltpu.VMEM((rows, CZ), F32)

    def message(rows):
        return jax.ShapeDtypeStruct((RANKS, rows, CZ), BF16)

    def message_vmem(rows):
        return pltpu.VMEM((RANKS, rows, CZ), BF16)

    def exchange(rows_of_ranks):
        return lax.all_to_all(rows_of_ranks, "mode", 0, 0, tiled=True)

    send, part = call(
        inner_kernel,
        (message(SENT), jax.ShapeDtypeStruct((4, SENT, CZ), F32)),
        [vmem()] + [hbm()] * 4,
        [rows_vmem(2 * MODES * SPACED + 2 * PAD), rows_vmem(SLAB), rows_vmem(SLAB)]
        + [rows_vmem(SLAB + PAD)] * 3
        + [rows_vmem(RANKS * STRIDE), message_vmem(SENT), dma((2, MODES)), dma((2,)), dma((RANKS,)), dma((4,))],
        "inner_images",
        size * 20,
        size * 14,
    )(table, mean_cond, pressure, source, concentration)
    send = call(
        outer_kernel,
        message(SENT),
        [hbm()] * 4,
        [
            rows_vmem(4 * STRIDE),
            halo_vmem,
            halo_vmem,
            rows_vmem(2 * CY),
            pltpu.VMEM((4, SENT, CZ), BF16),
            dma((6,)),
            dma((4,)),
        ],
        "outer_images",
        size,
        size,
        {3: 0},
    )(part, low, high, send)
    recv = exchange(send)

    base_p, base_c = call(
        base_kernel,
        (field, field),
        [smem(), smem()] + [hbm()] * 6,
        [rows_vmem(2 * MODES * SPACED + 2 * PAD), field_vmem, rows_vmem(SLAB), halo_vmem, halo_vmem]
        + [field_vmem, field_vmem, rows_vmem(SLAB), dma((4 + 2 * MODES,)), dma((2,))],
        "base",
        size * 60,
        size * 24,
    )(rank.reshape(1), table, pressure, source, concentration, mean_cond, low, high)

    recv, base_p, base_c = lax.optimization_barrier((recv, base_p, base_c))

    code = jnp.sum(table * POWERS.astype(np.int32)[:, None], axis=0)
    row = jnp.sum(jnp.where(code[None, :] == CODES[:, None], jnp.arange(ALL, dtype=jnp.int32)[None, :], 0), axis=1)
    places = row // MODES * STRIDE + row % MODES * SHARE
    places = jnp.concatenate([places, row[:1] // MODES * STRIDE])

    def share(rows):
        rows = lax.dynamic_slice_in_dim(rows, rank * SHARE, SHARE, rows.ndim - 2)
        return jnp.pad(rows, [(0, 0)] * (rows.ndim - 2) + [(0, FULL - SHARE), (0, 0)], constant_values=1.0)

    own_kl, own_mean = share(kl_cond), share(mean_cond)

    def contract(index):
        rows = ROWS if index else ROWS_HEAD
        return call(
            functools.partial(contract_kernel, index),
            message(rows),
            [smem()] + [hbm()] * 3,
            [
                message_vmem(SENT),
                pltpu.VMEM((KL, FULL, CZ), F32),
                rows_vmem(FULL),
                rows_vmem(RANKS * STRIDE),
                rows_vmem(VALID * FULL),
                pltpu.VMEM((ORDER * KL, FULL, CZ), F32),
                rows_vmem(RANKS * STRIDE),
                message_vmem(rows),
                dma((2, RANKS)),
                dma((2,)),
                dma((RANKS,)),
            ],
            "contract_concentration" if index else "contract_pressure",
            size * 40,
            size * 8,
        )(places, recv, own_kl, own_mean)

    back_p = exchange(contract(0))
    back_c = exchange(contract(1))

    def result(index, received, base):
        rows = ROWS if index else ROWS_HEAD
        return call(
            functools.partial(result_kernel, index),
            field if index else (field, plane),
            [hbm()] * 3,
            [message_vmem(rows), rows_vmem(MODES * SPACED), rows_vmem(SLAB), rows_vmem(SLAB + PAD)]
            + [rows_vmem(RANKS * (rows + PAD)), rows_vmem(SLAB + PAD), rows_vmem(MODES * SPACED)]
            + [dma((RANKS,)), dma((MODES,)), dma((MODES,)), dma((2,))],
            "concentration_result" if index else "pressure_result",
            size * 4,
            size * 10,
        )(received, base, mean_cond)

    pressure_next, head = result(0, back_p, base_p)
    head_low = lax.ppermute(head[-CY:], "space", up)
    head_high = lax.ppermute(head[:CY], "space", down)
    moved = call(
        advection_kernel,
        field,
        [hbm()] * 8,
        [rows_vmem(MODES * SLAB + 2 * PAD), halo_vmem, halo_vmem, field_vmem, rows_vmem(SLAB)]
        + [rows_vmem(SLAB + 2 * PAD), edge_vmem, edge_vmem, field_vmem, pltpu.VMEM((3, SLAB, CZ), F32)]
        + [dma((7 + MODES,)), dma((MODES,))],
        "advection",
        size * 20,
        size * 12,
    )(concentration, low, high, base_c, mean_cond, head, head_low, head_high)
    concentration_next = result(1, back_c, moved)
    return (pressure_next.reshape(shape), concentration_next.reshape(shape))


def solution(mesh):
    return jax.shard_map(
        local,
        mesh=mesh,
        in_specs=(
            P("mode", "space", None, None),
            P("mode", "space", None, None),
            P("mode", "space", None, None),
            P("space", None, None),
            P(None, "space", None, None),
            P(),
        ),
        out_specs=(P("mode", "space", None, None), P("mode", "space", None, None)),
        check_vma=False,
    )
```

```python
import functools
import itertools

import jax
import jax.numpy as jnp
import numpy as np
from jax import lax
from jax.experimental import pallas as pl
from jax.experimental.pallas import tpu as pltpu
from jax.sharding import PartitionSpec as P

OMEGA = 0.8
DISPERSION = 0.01
STEP = 0.05
ORDER = 3

F32 = jnp.float32
BF16 = jnp.bfloat16

RANKS = 16
MODES = 11
PLANES = 11
CY = 32
CZ = 128
KL = 8
ALL = RANKS * MODES
SLAB = PLANES * CY
SHARE = SLAB // RANKS
FULL = 24
BODY = SHARE * MODES
PAD = 8
SPACED = SLAB + PAD

SENT = 496
STRIDE = SENT + PAD

EDGE_RANKS = (0, 1, RANKS - 2, RANKS - 1)
LIMIT = 63 * 1024 * 1024

INDICES = sorted(
    (t for t in itertools.product(range(ORDER + 1), repeat=KL) if sum(t) <= ORDER), key=lambda t: (sum(t), t)
)
PLACE = {t: i for i, t in enumerate(INDICES)}
NEIGHBOURS = [
    [
        (d, max(t[d], t[d] + step), PLACE[t[:d] + (t[d] + step,) + t[d + 1 :]])
        for d in range(KL)
        for step in (-1, 1)
        if t[:d] + (t[d] + step,) + t[d + 1 :] in PLACE
    ]
    for t in INDICES
]
VALID = len(INDICES)
POWERS = (ORDER + 1) ** np.arange(KL)
CODES = (np.array(INDICES) * POWERS).sum(axis=1).astype(np.int32)


def vmem():
    return pl.BlockSpec(memory_space=pltpu.VMEM)


def smem():
    return pl.BlockSpec(memory_space=pltpu.SMEM)


def hbm():
    return pl.BlockSpec(memory_space=pltpu.HBM)


def call(kernel, outs, ins, scratch, name, flops, moved, aliases=None):
    return pl.pallas_call(
        kernel,
        out_shape=outs,
        in_specs=ins,
        out_specs=jax.tree.map(lambda _: hbm(), outs),
        scratch_shapes=scratch,
        input_output_aliases=aliases or {},
        compiler_params=pltpu.CompilerParams(vmem_limit_bytes=LIMIT),
        cost_estimate=pl.CostEstimate(flops=flops, bytes_accessed=moved, transcendentals=0),
        name=name,
    )


def start_all(sems, pairs):
    copies = [pltpu.make_async_copy(source, target, sems.at[i]) for i, (source, target) in enumerate(pairs)]
    for copy in copies:
        copy.start()
    return copies


def loop(first, last, work):
    def one(i, carry):
        work(i)
        return carry

    lax.fori_loop(first, last, one, 0)


def edge_masks():
    row = lax.broadcasted_iota(jnp.int32, (CY, CZ), 0)
    lane = lax.broadcasted_iota(jnp.int32, (CY, CZ), 1)
    return row == 0, row == CY - 1, lane == 0, lane == CZ - 1


def rows_of(ref, start):
    return ref[pl.ds(start, CY), :]


def beside(ref, start, tile, masks):
    first_row, last_row, first_lane, last_lane = masks
    y_less = jnp.where(first_row, 0.0, rows_of(ref, start - 1))
    y_more = jnp.where(last_row, 0.0, rows_of(ref, start + 1))
    z_less = jnp.where(first_lane, 0.0, pltpu.roll(tile, 1, 1))
    z_more = jnp.where(last_lane, 0.0, pltpu.roll(tile, CZ - 1, 1))
    return y_less, y_more, z_less, z_more


def laplace(ref, base, x, masks, outer=None):
    start = base + x * CY
    tile = rows_of(ref, start)
    y_less, y_more, z_less, z_more = beside(ref, start, tile, masks)
    total = (y_more + y_less) + (z_more + z_less)
    if x > 0:
        total = total + rows_of(ref, start - CY)
    if x < PLANES - 1:
        total = total + rows_of(ref, start + CY)
    if outer is not None:
        total = total + outer
    return tile, 6.0 * tile - total


def rounded(tile):
    return tile.astype(BF16).astype(F32)


def copy_share(target, to, source, start):
    for part in range(0, FULL, 8):
        target[pl.ds(to + part, 8), :] = source[pl.ds(start + part, 8), :]


def pack_rank(scratch, start, out_ref, slot, blocks):
    for block in range(blocks):
        out_ref[slot, pl.ds(block * 16, 16), :] = scratch[pl.ds(start + block * 16, 16), :].astype(BF16)


def unpack_rank(in_ref, rank, scratch, stride, blocks):
    for block in blocks:
        start = pl.multiple_of(rank * stride + block * 16, 8)
        scratch[pl.ds(start, 16), :] = in_ref[rank, pl.ds(block * 16, 16), :].astype(F32)


def inner_kernel(
    pressure_hbm, concentration_hbm, send_hbm, part_hbm, fields, image, scratch, strip, sems, send_sems, part_sems
):
    inputs = (pressure_hbm, concentration_hbm)

    def base_of(index, m):
        return pl.multiple_of(PAD + (index * MODES + m) * SPACED, 8)

    def fetch(index, m):
        target = fields.at[pl.ds(base_of(index, m), SLAB), :]
        return pltpu.make_async_copy(inputs[index].at[m], target, sems.at[index, m])

    for index in range(2):
        for m in range(MODES):
            fetch(index, m).start()
    for rank in range(RANKS):
        scratch[pl.ds(rank * STRIDE + 2 * BODY, SENT - 2 * BODY), :] = jnp.zeros((SENT - 2 * BODY, CZ), F32)
    masks = edge_masks()

    for index in range(2):

        def one_mode(m):
            fetch(index, m).wait()
            for x in range(PLANES):
                image[pl.ds(x * CY, CY), :] = laplace(fields, base_of(index, m), x, masks)[1]
            for rank in range(RANKS):
                copy_share(scratch, rank * STRIDE + (index * MODES + m) * SHARE, image, rank * SHARE)

        loop(0, MODES, one_mode)
    parts = start_all(
        part_sems,
        [(scratch.at[pl.ds(rank * STRIDE, SENT), :], part_hbm.at[i]) for i, rank in enumerate(EDGE_RANKS)],
    )

    def send(rank):
        return pltpu.make_async_copy(strip.at[rank], send_hbm.at[rank], send_sems.at[rank])

    def go(rank):
        pack_rank(scratch, pl.multiple_of(rank * STRIDE, 8), strip, rank, SENT // 16)
        send(rank).start()

    loop(2, RANKS - 2, go)
    for copy in parts:
        copy.wait()
    loop(2, RANKS - 2, lambda rank: send(rank).wait())


def outer_kernel(part_hbm, low_hbm, high_hbm, send_in, send_hbm, part, low, high, halo, strip, sems, send_sems):
    parts = [(part_hbm.at[i], part.at[pl.ds(i * STRIDE, SENT), :]) for i in range(4)]
    for copy in start_all(sems, parts + [(low_hbm, low), (high_hbm, high)]):
        copy.wait()

    def spread(mode):
        halo[pl.ds(0, CY), :] = low[mode].astype(F32)
        halo[pl.ds(CY, CY), :] = high[mode].astype(F32)
        row = mode * SHARE
        for i, at, of, count in (
            (0, 0, 0, SHARE),
            (1, 0, SHARE, CY - SHARE),
            (2, 2 * SHARE - CY, CY, CY - SHARE),
            (3, 0, 2 * CY - SHARE, SHARE),
        ):
            rows = pl.ds(i * STRIDE + row + at, count)
            part[rows, :] = part[rows, :] - halo[pl.ds(of, count), :]

    loop(0, 2 * MODES, spread)
    sends = []
    for i, rank in enumerate(EDGE_RANKS):
        pack_rank(part, i * STRIDE, strip, i, SENT // 16)
        send = pltpu.make_async_copy(strip.at[i], send_hbm.at[rank], send_sems.at[i])
        send.start()
        sends.append(send)
    for send in sends:
        send.wait()


def base_kernel(
    rank_ref, table_ref, pressure_hbm, source_hbm, concentration_hbm, mean_hbm, low_hbm, high_hbm,
    base_p_hbm, base_c_hbm,
    fields, source, mean, low, high, base_p, base_c, scale, sems, out_sems,
):
    copies = start_all(
        sems,
        [(mean_hbm, mean), (low_hbm, low), (high_hbm, high)]
        + [(pressure_hbm.at[m], fields.at[pl.ds(PAD + m * SPACED, SLAB), :]) for m in range(MODES)]
        + [(concentration_hbm.at[m], fields.at[pl.ds(PAD + (MODES + m) * SPACED, SLAB), :]) for m in range(MODES)]
        + [(source_hbm, source)],
    )
    for copy in copies:
        copy.wait()
    scale[...] = OMEGA / (6.0 * mean[...])
    masks = edge_masks()

    def one_mode(m):
        own = (table_ref[0, rank_ref[0] * MODES + m] >= 0).astype(F32)
        for index in range(2):
            base = pl.multiple_of(PAD + (index * MODES + m) * SPACED, 8)
            for x in range(PLANES):
                outer = None
                if x == 0:
                    outer = low[index * MODES + m].astype(F32)
                elif x == PLANES - 1:
                    outer = high[index * MODES + m].astype(F32)
                tile, image = laplace(fields, base, x, masks, outer)
                rows = pl.ds(x * CY, CY)
                term = own * (mean[rows, :] * rounded(image))
                if index == 0:
                    base_p[m, rows, :] = tile + scale[rows, :] * (source[m, rows, :] - term)
                else:
                    base_c[m, rows, :] = tile - DISPERSION * term

    loop(0, MODES, one_mode)
    for copy in start_all(out_sems, [(base_p, base_p_hbm), (base_c, base_c_hbm)]):
        copy.wait()


def head_kernel(
    rank_ref, table_ref, pressure_hbm, source_hbm, mean_hbm, kl_hbm, low_hbm, high_hbm, out_hbm,
    field, source, mean, kl, low, high, scale, out, sems, mean_sem, out_sem,
):
    fetch_mean = pltpu.make_async_copy(mean_hbm, mean, mean_sem)
    fetch_mean.start()
    out[...] = jnp.zeros((SLAB, CZ), F32)
    fetch_mean.wait()
    scale[...] = OMEGA / (6.0 * mean[...])
    masks = edge_masks()

    def one_mode(m):
        row = rank_ref[0] * MODES + m
        degree = table_ref[0, row]
        which = 0
        for d in range(1, KL):
            degree = degree + table_ref[d, row]
            which = which + d * table_ref[d, row]

        @pl.when((degree >= 0) & (degree <= 1))
        def _():
            copies = start_all(
                sems,
                [
                    (pressure_hbm.at[m], field.at[pl.ds(PAD, SLAB), :]),
                    (source_hbm.at[m], source),
                    (kl_hbm.at[which], kl),
                    (low_hbm.at[m], low),
                    (high_hbm.at[m], high),
                ],
            )
            for copy in copies:
                copy.wait()
            is_mean = (degree == 0).astype(F32)
            for x in range(PLANES):
                outer = None
                if x == 0:
                    outer = low[...].astype(F32)
                elif x == PLANES - 1:
                    outer = high[...].astype(F32)
                tile, image = laplace(field, PAD, x, masks, outer)
                image = rounded(image)
                rows = pl.ds(x * CY, CY)
                own = tile + scale[rows, :] * (source[rows, :] - mean[rows, :] * image)
                brought = scale[rows, :] * (kl[rows, :] * image)
                out[rows, :] = out[rows, :] + (is_mean * own - (1.0 - is_mean) * brought)

    loop(0, MODES, one_mode)
    leave = pltpu.make_async_copy(out, out_hbm, out_sem)
    leave.start()
    leave.wait()


def contract_kernel(
    places, recv_hbm, kl_hbm, send_hbm,
    recv, kl, images, ordered, weights, outs, strip, recv_sems, kl_sem, send_sems,
):
    def fetch(rank):
        return pltpu.make_async_copy(recv_hbm.at[rank], recv.at[rank], recv_sems.at[rank])

    loop(0, RANKS, lambda rank: fetch(rank).start())
    fetch_kl = pltpu.make_async_copy(kl_hbm, kl, kl_sem)
    fetch_kl.start()

    def clear(rank):
        outs[pl.ds(pl.multiple_of(rank * STRIDE, 8), SENT), :] = jnp.zeros((SENT, CZ), F32)

    loop(0, RANKS, clear)
    fetch_kl.wait()
    for larger in range(ORDER):
        root = float(np.sqrt(np.float32(larger + 1)).astype(jnp.bfloat16))
        for d in range(KL):
            weights[larger * KL + d] = root * kl[d]

    def spread(rank):
        fetch(rank).wait()
        unpack_rank(recv, rank, images, STRIDE, range(SENT // 16))

    loop(0, RANKS, spread)

    def one_field(index):
        for i in range(VALID):
            copy_share(ordered, i * FULL, images, places[i] + index * BODY)
        for part in range(0, FULL, 8):
            count = min(8, SHARE - part)
            held = [weights[i, pl.ds(part, 8), :] for i in range(ORDER * KL)]
            for i in range(VALID):
                total = None
                for d, larger, other in NEIGHBOURS[i]:
                    term = held[(larger - 1) * KL + d] * ordered[pl.ds(other * FULL + part, 8), :]
                    total = term if total is None else total + term
                outs[pl.ds(places[i] + index * BODY + part, count), :] = total[:count]

    loop(0, 2, one_field)

    def send(rank):
        return pltpu.make_async_copy(strip.at[rank], send_hbm.at[rank], send_sems.at[rank])

    def go(rank):
        pack_rank(outs, pl.multiple_of(rank * STRIDE, 8), strip, rank, SENT // 16)
        send(rank).start()

    loop(0, RANKS, go)
    loop(0, RANKS, lambda rank: send(rank).wait())


def result_kernel(
    recv_hbm, base_p_hbm, base_c_hbm, mean_hbm, out_p_hbm, out_c_hbm,
    recv, base, mean, scale, sums, out, recv_sems, base_sems, mean_sem, sems,
):
    bases = (base_p_hbm, base_c_hbm)
    outputs = (out_p_hbm, out_c_hbm)

    def fetch(rank):
        return pltpu.make_async_copy(recv_hbm.at[rank], recv.at[rank], recv_sems.at[rank])

    def rows_at(index, m):
        return pl.ds(pl.multiple_of((index * MODES + m) * SPACED, 8), SLAB)

    def fetch_base(index, m):
        return pltpu.make_async_copy(bases[index].at[m], base.at[rows_at(index, m), :], base_sems.at[index, m])

    def leave(index, m):
        return pltpu.make_async_copy(out.at[rows_at(index, m), :], outputs[index].at[m], sems.at[index, m])

    loop(0, RANKS, lambda rank: fetch(rank).start())
    fetch_mean = pltpu.make_async_copy(mean_hbm, mean, mean_sem)
    fetch_mean.start()
    for index in range(2):
        loop(0, MODES, lambda m: fetch_base(index, m).start())
    fetch_mean.wait()
    scale[pl.ds(0, SLAB), :] = OMEGA / (6.0 * mean[...])

    def spread(rank):
        fetch(rank).wait()
        unpack_rank(recv, rank, sums, STRIDE, range(SENT // 16))

    loop(0, RANKS, spread)
    for index in range(2):

        def one_mode(m):
            fetch_base(index, m).wait()
            for rank in range(RANKS):
                for part in range(0, FULL, 8):
                    at = pl.ds((index * MODES + m) * SPACED + rank * SHARE + part, 8)
                    factor = DISPERSION if index else scale[pl.ds(rank * SHARE + part, 8), :]
                    total = sums[pl.ds(rank * STRIDE + (index * MODES + m) * SHARE + part, 8), :]
                    out[at, :] = base[at, :] - factor * total
            leave(index, m).start()

        loop(0, MODES, one_mode)
    for index in range(2):
        loop(0, MODES, lambda m: leave(index, m).wait())


def advection_kernel(
    field_hbm, low_hbm, high_hbm, base_hbm, mean_hbm, head_hbm, head_low_hbm, head_high_hbm, out_hbm,
    field, low, high, base, mean, head, head_low, head_high, out, speed, sems, out_sems,
):
    copies = start_all(
        sems,
        [
            (head_hbm, head.at[pl.ds(PAD, SLAB), :]),
            (head_low_hbm, head_low),
            (head_high_hbm, head_high),
            (mean_hbm, mean),
            (low_hbm, low),
            (high_hbm, high),
            (base_hbm, base),
        ]
        + [(field_hbm.at[m], field.at[pl.ds(PAD + m * SLAB, SLAB), :]) for m in range(MODES)],
    )
    masks = edge_masks()

    def steps(ref, base, x, outer):
        start = base + x * CY
        below = rows_of(ref, start - CY) if x > 0 else outer(0)
        above = rows_of(ref, start + CY) if x < PLANES - 1 else outer(1)
        y_less, y_more, z_less, z_more = beside(ref, start, rows_of(ref, start), masks)
        return above - below, y_more - y_less, z_more - z_less

    for copy in copies[:4]:
        copy.wait()
    for x in range(PLANES):
        rows = pl.ds(x * CY, CY)
        factor = (0.25 * STEP) * mean[rows, :]
        for axis, step in enumerate(steps(head, PAD, x, lambda side: (head_low, head_high)[side][...])):
            speed[axis, rows, :] = factor * step
    for copy in copies[4:]:
        copy.wait()

    def leave(m):
        return pltpu.make_async_copy(out.at[m], out_hbm.at[m], out_sems.at[m])

    def one_mode(m):
        for x in range(PLANES):
            rows = pl.ds(x * CY, CY)
            along = steps(
                field, pl.multiple_of(PAD + m * SLAB, 8), x, lambda side: (low, high)[side][MODES + m].astype(F32)
            )
            moved = sum(speed[axis, rows, :] * step for axis, step in enumerate(along))
            out[m, rows, :] = base[m, rows, :] + moved
        leave(m).start()

    loop(0, MODES, one_mode)
    loop(0, MODES, lambda m: leave(m).wait())


def local(pressure, source, concentration, mean_cond, kl_cond, mode_table):
    shape = pressure.shape
    spaces = lax.axis_size("space")
    up = [(i, i + 1) for i in range(spaces - 1)]
    down = [(i + 1, i) for i in range(spaces - 1)]
    rank = lax.axis_index("mode").astype(jnp.int32)
    table = mode_table.T
    size = pressure.size
    last = jnp.concatenate([pressure[:, -1], concentration[:, -1]], axis=0).astype(BF16)
    first = jnp.concatenate([pressure[:, 0], concentration[:, 0]], axis=0).astype(BF16)
    low = lax.ppermute(last, "space", up)
    high = lax.ppermute(first, "space", down)

    pressure, source, concentration = (a.reshape(MODES, SLAB, CZ) for a in (pressure, source, concentration))
    mean_cond = mean_cond.reshape(SLAB, CZ)
    kl_cond = kl_cond.reshape(KL, SLAB, CZ)

    field = jax.ShapeDtypeStruct(pressure.shape, F32)
    plane = jax.ShapeDtypeStruct(mean_cond.shape, F32)
    dma = pltpu.SemaphoreType.DMA
    field_vmem = pltpu.VMEM(pressure.shape, F32)
    halo_vmem = pltpu.VMEM((2 * MODES, CY, CZ), BF16)
    edge_vmem = pltpu.VMEM((CY, CZ), F32)

    def rows_vmem(rows):
        return pltpu.VMEM((rows, CZ), F32)

    def message(rows):
        return jax.ShapeDtypeStruct((RANKS, rows, CZ), BF16)

    def message_vmem(rows):
        return pltpu.VMEM((RANKS, rows, CZ), BF16)

    def exchange(rows_of_ranks):
        return lax.all_to_all(rows_of_ranks, "mode", 0, 0, tiled=True)

    send, part = call(
        inner_kernel,
        (message(SENT), jax.ShapeDtypeStruct((4, SENT, CZ), F32)),
        [hbm()] * 2,
        [rows_vmem(2 * MODES * SPACED + 2 * PAD), rows_vmem(SLAB + PAD), rows_vmem(RANKS * STRIDE), message_vmem(SENT)]
        + [dma((2, MODES)), dma((RANKS,)), dma((4,))],
        "inner_images",
        size * 20,
        size * 14,
    )(pressure, concentration)
    send = call(
        outer_kernel,
        message(SENT),
        [hbm()] * 4,
        [
            rows_vmem(4 * STRIDE),
            halo_vmem,
            halo_vmem,
            rows_vmem(2 * CY),
            pltpu.VMEM((4, SENT, CZ), BF16),
            dma((6,)),
            dma((4,)),
        ],
        "outer_images",
        size,
        size,
        {3: 0},
    )(part, low, high, send)
    recv = exchange(send)

    own_rank = rank.reshape(1)
    head = call(
        head_kernel,
        plane,
        [smem(), smem()] + [hbm()] * 6,
        [rows_vmem(SLAB + 2 * PAD)] + [rows_vmem(SLAB)] * 3
        + [pltpu.VMEM((CY, CZ), BF16)] * 2 + [rows_vmem(SLAB)] * 2 + [dma((5,)), dma(()), dma(())],
        "head_part",
        size,
        size,
    )(own_rank, table, pressure, source, mean_cond, kl_cond, low, high)

    def partner(rows, bits):
        return lax.ppermute(rows, "mode", [(i, i ^ bits) for i in range(RANKS)])

    core = rank % 2
    half = SLAB // 2
    kept = lax.dynamic_slice_in_dim(head, core * half, half, 0)
    kept = kept + partner(lax.dynamic_slice_in_dim(head, (1 - core) * half, half, 0), 1)
    kept = kept + partner(kept, 2)

    base_p, base_c = call(
        base_kernel,
        (field, field),
        [smem(), smem()] + [hbm()] * 6,
        [rows_vmem(2 * MODES * SPACED + 2 * PAD), field_vmem, rows_vmem(SLAB), halo_vmem, halo_vmem]
        + [field_vmem, field_vmem, rows_vmem(SLAB), dma((4 + 2 * MODES,)), dma((2,))],
        "base",
        size * 60,
        size * 24,
    )(own_rank, table, pressure, source, concentration, mean_cond, low, high)

    recv, base_p, base_c, kept = lax.optimization_barrier((recv, base_p, base_c, kept))

    code = jnp.sum(table * POWERS.astype(np.int32)[:, None], axis=0)
    row = jnp.sum(jnp.where(code[None, :] == CODES[:, None], jnp.arange(ALL, dtype=jnp.int32)[None, :], 0), axis=1)
    places = row // MODES * STRIDE + row % MODES * SHARE

    own_kl = lax.dynamic_slice_in_dim(kl_cond, rank * SHARE, SHARE, 1)
    own_kl = jnp.pad(own_kl, ((0, 0), (0, FULL - SHARE), (0, 0)))

    back = call(
        contract_kernel,
        message(SENT),
        [smem()] + [hbm()] * 2,
        [
            message_vmem(SENT),
            pltpu.VMEM((KL, FULL, CZ), F32),
            rows_vmem(RANKS * STRIDE),
            rows_vmem(VALID * FULL),
            pltpu.VMEM((ORDER * KL, FULL, CZ), F32),
            rows_vmem(RANKS * STRIDE),
            message_vmem(SENT),
            dma((RANKS,)),
            dma(()),
            dma((RANKS,)),
        ],
        "contract",
        size * 80,
        size * 16,
    )(places, recv, own_kl)
    kept = (kept + partner(kept, 4)) + (partner(kept, 8) + partner(kept, 12))
    back, kept = lax.optimization_barrier((back, kept))
    received = exchange(back)

    other = partner(kept, 1)
    first_half = jnp.where(core == 0, kept, other)
    second_half = jnp.where(core == 0, other, kept)
    head = jnp.concatenate([first_half, second_half], axis=0)
    head_low = lax.ppermute(head[-CY:], "space", up)
    head_high = lax.ppermute(head[:CY], "space", down)
    moved = call(
        advection_kernel,
        field,
        [hbm()] * 8,
        [rows_vmem(MODES * SLAB + 2 * PAD), halo_vmem, halo_vmem, field_vmem, rows_vmem(SLAB)]
        + [rows_vmem(SLAB + 2 * PAD), edge_vmem, edge_vmem, field_vmem, pltpu.VMEM((3, SLAB, CZ), F32)]
        + [dma((7 + MODES,)), dma((MODES,))],
        "advection",
        size * 20,
        size * 12,
    )(concentration, low, high, base_c, mean_cond, head, head_low, head_high)
    pressure_next, concentration_next = call(
        result_kernel,
        (field, field),
        [hbm()] * 4,
        [message_vmem(SENT), rows_vmem(2 * MODES * SPACED), rows_vmem(SLAB), rows_vmem(SLAB + PAD)]
        + [rows_vmem(RANKS * STRIDE), rows_vmem(2 * MODES * SPACED)]
        + [dma((RANKS,)), dma((2, MODES)), dma(()), dma((2, MODES))],
        "result",
        size * 8,
        size * 20,
    )(received, base_p, moved, mean_cond)
    return (pressure_next.reshape(shape), concentration_next.reshape(shape))


def solution(mesh):
    return jax.shard_map(
        local,
        mesh=mesh,
        in_specs=(
            P("mode", "space", None, None),
            P("mode", "space", None, None),
            P("mode", "space", None, None),
            P("space", None, None),
            P(None, "space", None, None),
            P(),
        ),
        out_specs=(P("mode", "space", None, None), P("mode", "space", None, None)),
        check_vma=False,
    )
```

```python
import functools
import itertools

import jax
import jax.numpy as jnp
import numpy as np
from jax import lax
from jax.experimental import pallas as pl
from jax.experimental.pallas import tpu as pltpu
from jax.sharding import PartitionSpec as P

OMEGA = 0.8
DISPERSION = 0.01
STEP = 0.05
ORDER = 3

F32 = jnp.float32
BF16 = jnp.bfloat16

RANKS = 16
MODES = 11
PLANES = 11
CY = 32
CZ = 128
KL = 8
ALL = RANKS * MODES
SLAB = PLANES * CY
SHARE = SLAB // RANKS
FULL = 24
BODY = SHARE * MODES
PAD = 8
SPACED = SLAB + PAD

SENT = 496
STRIDE = SENT + PAD

EDGE_RANKS = (0, 1, RANKS - 2, RANKS - 1)
LIMIT = 63 * 1024 * 1024

INDICES = sorted(
    (t for t in itertools.product(range(ORDER + 1), repeat=KL) if sum(t) <= ORDER), key=lambda t: (sum(t), t)
)
PLACE = {t: i for i, t in enumerate(INDICES)}
NEIGHBOURS = [
    [
        (d, max(t[d], t[d] + step), PLACE[t[:d] + (t[d] + step,) + t[d + 1 :]])
        for d in range(KL)
        for step in (-1, 1)
        if t[:d] + (t[d] + step,) + t[d + 1 :] in PLACE
    ]
    for t in INDICES
]
VALID = len(INDICES)
POWERS = (ORDER + 1) ** np.arange(KL)
CODES = (np.array(INDICES) * POWERS).sum(axis=1).astype(np.int32)


def vmem():
    return pl.BlockSpec(memory_space=pltpu.VMEM)


def smem():
    return pl.BlockSpec(memory_space=pltpu.SMEM)


def hbm():
    return pl.BlockSpec(memory_space=pltpu.HBM)


def call(kernel, outs, ins, scratch, name, flops, moved, aliases=None):
    return pl.pallas_call(
        kernel,
        out_shape=outs,
        in_specs=ins,
        out_specs=jax.tree.map(lambda _: hbm(), outs),
        scratch_shapes=scratch,
        input_output_aliases=aliases or {},
        compiler_params=pltpu.CompilerParams(vmem_limit_bytes=LIMIT),
        cost_estimate=pl.CostEstimate(flops=flops, bytes_accessed=moved, transcendentals=0),
        name=name,
    )


def start_all(sems, pairs):
    copies = [pltpu.make_async_copy(source, target, sems.at[i]) for i, (source, target) in enumerate(pairs)]
    for copy in copies:
        copy.start()
    return copies


def loop(first, last, work):
    def one(i, carry):
        work(i)
        return carry

    lax.fori_loop(first, last, one, 0)


def edge_masks():
    row = lax.broadcasted_iota(jnp.int32, (CY, CZ), 0)
    lane = lax.broadcasted_iota(jnp.int32, (CY, CZ), 1)
    return row == 0, row == CY - 1, lane == 0, lane == CZ - 1


def rows_of(ref, start):
    return ref[pl.ds(start, CY), :]


def beside(ref, start, tile, masks):
    first_row, last_row, first_lane, last_lane = masks
    y_less = jnp.where(first_row, 0.0, rows_of(ref, start - 1))
    y_more = jnp.where(last_row, 0.0, rows_of(ref, start + 1))
    z_less = jnp.where(first_lane, 0.0, pltpu.roll(tile, 1, 1))
    z_more = jnp.where(last_lane, 0.0, pltpu.roll(tile, CZ - 1, 1))
    return y_less, y_more, z_less, z_more


def laplace(ref, base, x, masks, outer=None):
    start = base + x * CY
    tile = rows_of(ref, start)
    y_less, y_more, z_less, z_more = beside(ref, start, tile, masks)
    total = (y_more + y_less) + (z_more + z_less)
    if x > 0:
        total = total + rows_of(ref, start - CY)
    if x < PLANES - 1:
        total = total + rows_of(ref, start + CY)
    if outer is not None:
        total = total + outer
    return tile, 6.0 * tile - total


def rounded(tile):
    return tile.astype(BF16).astype(F32)


def copy_share(target, to, source, start):
    for part in range(0, FULL, 8):
        target[pl.ds(to + part, 8), :] = source[pl.ds(start + part, 8), :]


def pack_rank(scratch, start, out_ref, slot, blocks):
    for block in range(blocks):
        out_ref[slot, pl.ds(block * 16, 16), :] = scratch[pl.ds(start + block * 16, 16), :].astype(BF16)


def unpack_rank(in_ref, rank, scratch, stride, blocks):
    for block in blocks:
        start = pl.multiple_of(rank * stride + block * 16, 8)
        scratch[pl.ds(start, 16), :] = in_ref[rank, pl.ds(block * 16, 16), :].astype(F32)


def inner_kernel(
    pressure_hbm, concentration_hbm, send_hbm, part_hbm, fields, image, scratch, strip, sems, send_sems, part_sems
):
    inputs = (pressure_hbm, concentration_hbm)

    def base_of(index, m):
        return pl.multiple_of(PAD + (index * MODES + m) * SPACED, 8)

    def fetch(index, m):
        target = fields.at[pl.ds(base_of(index, m), SLAB), :]
        return pltpu.make_async_copy(inputs[index].at[m], target, sems.at[index, m])

    for index in range(2):
        for m in range(MODES):
            fetch(index, m).start()
    for rank in range(RANKS):
        scratch[pl.ds(rank * STRIDE + 2 * BODY, SENT - 2 * BODY), :] = jnp.zeros((SENT - 2 * BODY, CZ), F32)
    masks = edge_masks()

    for index in range(2):

        def one_mode(m):
            fetch(index, m).wait()
            for x in range(PLANES):
                image[pl.ds(x * CY, CY), :] = laplace(fields, base_of(index, m), x, masks)[1]
            for rank in range(RANKS):
                copy_share(scratch, rank * STRIDE + (index * MODES + m) * SHARE, image, rank * SHARE)

        loop(0, MODES, one_mode)
    parts = start_all(
        part_sems,
        [(scratch.at[pl.ds(rank * STRIDE, SENT), :], part_hbm.at[i]) for i, rank in enumerate(EDGE_RANKS)],
    )

    def send(rank):
        return pltpu.make_async_copy(strip.at[rank], send_hbm.at[rank], send_sems.at[rank])

    def go(rank):
        pack_rank(scratch, pl.multiple_of(rank * STRIDE, 8), strip, rank, SENT // 16)
        send(rank).start()

    loop(2, RANKS - 2, go)
    for copy in parts:
        copy.wait()
    loop(2, RANKS - 2, lambda rank: send(rank).wait())


def outer_kernel(part_hbm, low_hbm, high_hbm, send_in, send_hbm, part, low, high, halo, strip, sems, send_sems):
    parts = [(part_hbm.at[i], part.at[pl.ds(i * STRIDE, SENT), :]) for i in range(4)]
    for copy in start_all(sems, parts + [(low_hbm, low), (high_hbm, high)]):
        copy.wait()

    def spread(mode):
        halo[pl.ds(0, CY), :] = low[mode].astype(F32)
        halo[pl.ds(CY, CY), :] = high[mode].astype(F32)
        row = mode * SHARE
        for i, at, of, count in (
            (0, 0, 0, SHARE),
            (1, 0, SHARE, CY - SHARE),
            (2, 2 * SHARE - CY, CY, CY - SHARE),
            (3, 0, 2 * CY - SHARE, SHARE),
        ):
            rows = pl.ds(i * STRIDE + row + at, count)
            part[rows, :] = part[rows, :] - halo[pl.ds(of, count), :]

    loop(0, 2 * MODES, spread)
    sends = []
    for i, rank in enumerate(EDGE_RANKS):
        pack_rank(part, i * STRIDE, strip, i, SENT // 16)
        send = pltpu.make_async_copy(strip.at[i], send_hbm.at[rank], send_sems.at[i])
        send.start()
        sends.append(send)
    for send in sends:
        send.wait()


def base_kernel(
    rank_ref, table_ref, pressure_hbm, source_hbm, concentration_hbm, mean_hbm, low_hbm, high_hbm,
    base_p_hbm, base_c_hbm,
    fields, source, mean, low, high, base_p, base_c, scale, sems, out_sems,
):
    copies = start_all(
        sems,
        [(mean_hbm, mean), (low_hbm, low), (high_hbm, high)]
        + [(pressure_hbm.at[m], fields.at[pl.ds(PAD + m * SPACED, SLAB), :]) for m in range(MODES)]
        + [(concentration_hbm.at[m], fields.at[pl.ds(PAD + (MODES + m) * SPACED, SLAB), :]) for m in range(MODES)]
        + [(source_hbm, source)],
    )
    for copy in copies:
        copy.wait()
    scale[...] = OMEGA / (6.0 * mean[...])
    masks = edge_masks()

    def one_mode(m):
        own = (table_ref[0, rank_ref[0] * MODES + m] >= 0).astype(F32)
        for index in range(2):
            base = pl.multiple_of(PAD + (index * MODES + m) * SPACED, 8)
            for x in range(PLANES):
                outer = None
                if x == 0:
                    outer = low[index * MODES + m].astype(F32)
                elif x == PLANES - 1:
                    outer = high[index * MODES + m].astype(F32)
                tile, image = laplace(fields, base, x, masks, outer)
                rows = pl.ds(x * CY, CY)
                term = own * (mean[rows, :] * rounded(image))
                if index == 0:
                    base_p[m, rows, :] = tile + scale[rows, :] * (source[m, rows, :] - term)
                else:
                    base_c[m, rows, :] = tile - DISPERSION * term

    loop(0, MODES, one_mode)
    for copy in start_all(out_sems, [(base_p, base_p_hbm), (base_c, base_c_hbm)]):
        copy.wait()


def head_kernel(
    rank_ref, table_ref, pressure_hbm, source_hbm, mean_hbm, kl_hbm, low_hbm, high_hbm, out_hbm,
    field, source, mean, kl, low, high, scale, out, sems, mean_sem, out_sem,
):
    fetch_mean = pltpu.make_async_copy(mean_hbm, mean, mean_sem)
    fetch_mean.start()
    out[...] = jnp.zeros((SLAB, CZ), F32)
    fetch_mean.wait()
    scale[...] = OMEGA / (6.0 * mean[...])
    masks = edge_masks()

    def one_mode(m):
        row = rank_ref[0] * MODES + m
        degree = table_ref[0, row]
        which = 0
        for d in range(1, KL):
            degree = degree + table_ref[d, row]
            which = which + d * table_ref[d, row]

        @pl.when((degree >= 0) & (degree <= 1))
        def _():
            copies = start_all(
                sems,
                [
                    (pressure_hbm.at[m], field.at[pl.ds(PAD, SLAB), :]),
                    (source_hbm.at[m], source),
                    (kl_hbm.at[which], kl),
                    (low_hbm.at[m], low),
                    (high_hbm.at[m], high),
                ],
            )
            for copy in copies:
                copy.wait()
            is_mean = (degree == 0).astype(F32)
            for x in range(PLANES):
                outer = None
                if x == 0:
                    outer = low[...].astype(F32)
                elif x == PLANES - 1:
                    outer = high[...].astype(F32)
                tile, image = laplace(field, PAD, x, masks, outer)
                image = rounded(image)
                rows = pl.ds(x * CY, CY)
                own = tile + scale[rows, :] * (source[rows, :] - mean[rows, :] * image)
                brought = scale[rows, :] * (kl[rows, :] * image)
                out[rows, :] = out[rows, :] + (is_mean * own - (1.0 - is_mean) * brought)

    loop(0, MODES, one_mode)
    leave = pltpu.make_async_copy(out, out_hbm, out_sem)
    leave.start()
    leave.wait()


def contract_kernel(
    places, recv_hbm, kl_hbm, send_hbm,
    recv, kl, images, ordered, weights, outs, strip, recv_sems, kl_sem, send_sems,
):
    def fetch(rank):
        return pltpu.make_async_copy(recv_hbm.at[rank], recv.at[rank], recv_sems.at[rank])

    loop(0, RANKS, lambda rank: fetch(rank).start())
    fetch_kl = pltpu.make_async_copy(kl_hbm, kl, kl_sem)
    fetch_kl.start()

    def clear(rank):
        outs[pl.ds(pl.multiple_of(rank * STRIDE, 8), SENT), :] = jnp.zeros((SENT, CZ), F32)

    loop(0, RANKS, clear)
    fetch_kl.wait()
    for larger in range(ORDER):
        root = float(np.sqrt(np.float32(larger + 1)).astype(jnp.bfloat16))
        for d in range(KL):
            weights[larger * KL + d] = root * kl[d]

    def spread(rank):
        fetch(rank).wait()
        unpack_rank(recv, rank, images, STRIDE, range(SENT // 16))

    loop(0, RANKS, spread)

    def one_field(index):
        for i in range(VALID):
            copy_share(ordered, i * FULL, images, places[i] + index * BODY)
        for part in range(0, FULL, 8):
            count = min(8, SHARE - part)
            held = [weights[i, pl.ds(part, 8), :] for i in range(ORDER * KL)]
            for i in range(VALID):
                total = None
                for d, larger, other in NEIGHBOURS[i]:
                    term = held[(larger - 1) * KL + d] * ordered[pl.ds(other * FULL + part, 8), :]
                    total = term if total is None else total + term
                outs[pl.ds(places[i] + index * BODY + part, count), :] = total[:count]

    loop(0, 2, one_field)

    def send(rank):
        return pltpu.make_async_copy(strip.at[rank], send_hbm.at[rank], send_sems.at[rank])

    def go(rank):
        pack_rank(outs, pl.multiple_of(rank * STRIDE, 8), strip, rank, SENT // 16)
        send(rank).start()

    loop(0, RANKS, go)
    loop(0, RANKS, lambda rank: send(rank).wait())


def result_kernel(
    recv_hbm, base_p_hbm, base_c_hbm, mean_hbm, out_p_hbm, out_c_hbm,
    recv, base, mean, scale, sums, out, recv_sems, base_sems, mean_sem, sems,
):
    bases = (base_p_hbm, base_c_hbm)
    outputs = (out_p_hbm, out_c_hbm)

    def fetch(rank):
        return pltpu.make_async_copy(recv_hbm.at[rank], recv.at[rank], recv_sems.at[rank])

    def rows_at(index, m):
        return pl.ds(pl.multiple_of((index * MODES + m) * SPACED, 8), SLAB)

    def fetch_base(index, m):
        return pltpu.make_async_copy(bases[index].at[m], base.at[rows_at(index, m), :], base_sems.at[index, m])

    def leave(index, m):
        return pltpu.make_async_copy(out.at[rows_at(index, m), :], outputs[index].at[m], sems.at[index, m])

    loop(0, RANKS, lambda rank: fetch(rank).start())
    fetch_mean = pltpu.make_async_copy(mean_hbm, mean, mean_sem)
    fetch_mean.start()
    for index in range(2):
        loop(0, MODES, lambda m: fetch_base(index, m).start())
    fetch_mean.wait()
    scale[pl.ds(0, SLAB), :] = OMEGA / (6.0 * mean[...])

    def spread(rank):
        fetch(rank).wait()
        unpack_rank(recv, rank, sums, STRIDE, range(SENT // 16))

    loop(0, RANKS, spread)
    for index in range(2):

        def one_mode(m):
            fetch_base(index, m).wait()
            for rank in range(RANKS):
                for part in range(0, FULL, 8):
                    at = pl.ds((index * MODES + m) * SPACED + rank * SHARE + part, 8)
                    factor = DISPERSION if index else scale[pl.ds(rank * SHARE + part, 8), :]
                    total = sums[pl.ds(rank * STRIDE + (index * MODES + m) * SHARE + part, 8), :]
                    out[at, :] = base[at, :] - factor * total
            leave(index, m).start()

        loop(0, MODES, one_mode)
    for index in range(2):
        loop(0, MODES, lambda m: leave(index, m).wait())


def advection_kernel(
    field_hbm, low_hbm, high_hbm, base_hbm, mean_hbm, head_hbm, head_low_hbm, head_high_hbm, out_hbm,
    field, low, high, base, mean, head, head_low, head_high, out, speed, sems, out_sems,
):
    copies = start_all(
        sems,
        [
            (head_hbm, head.at[pl.ds(PAD, SLAB), :]),
            (head_low_hbm, head_low),
            (head_high_hbm, head_high),
            (mean_hbm, mean),
            (low_hbm, low),
            (high_hbm, high),
            (base_hbm, base),
        ]
        + [(field_hbm.at[m], field.at[pl.ds(PAD + m * SLAB, SLAB), :]) for m in range(MODES)],
    )
    masks = edge_masks()

    def steps(ref, base, x, outer):
        start = base + x * CY
        below = rows_of(ref, start - CY) if x > 0 else outer(0)
        above = rows_of(ref, start + CY) if x < PLANES - 1 else outer(1)
        y_less, y_more, z_less, z_more = beside(ref, start, rows_of(ref, start), masks)
        return above - below, y_more - y_less, z_more - z_less

    for copy in copies[:4]:
        copy.wait()
    for x in range(PLANES):
        rows = pl.ds(x * CY, CY)
        factor = (0.25 * STEP) * mean[rows, :]
        for axis, step in enumerate(steps(head, PAD, x, lambda side: (head_low, head_high)[side][...])):
            speed[axis, rows, :] = factor * step
    for copy in copies[4:]:
        copy.wait()

    def leave(m):
        return pltpu.make_async_copy(out.at[m], out_hbm.at[m], out_sems.at[m])

    def one_mode(m):
        for x in range(PLANES):
            rows = pl.ds(x * CY, CY)
            along = steps(
                field, pl.multiple_of(PAD + m * SLAB, 8), x, lambda side: (low, high)[side][MODES + m].astype(F32)
            )
            moved = sum(speed[axis, rows, :] * step for axis, step in enumerate(along))
            out[m, rows, :] = base[m, rows, :] + moved
        leave(m).start()

    loop(0, MODES, one_mode)
    loop(0, MODES, lambda m: leave(m).wait())


def local(pressure, source, concentration, mean_cond, kl_cond, mode_table):
    shape = pressure.shape
    spaces = lax.axis_size("space")
    up = [(i, i + 1) for i in range(spaces - 1)]
    down = [(i + 1, i) for i in range(spaces - 1)]
    rank = lax.axis_index("mode").astype(jnp.int32)
    table = mode_table.T
    size = pressure.size
    last = jnp.concatenate([pressure[:, -1], concentration[:, -1]], axis=0).astype(BF16)
    first = jnp.concatenate([pressure[:, 0], concentration[:, 0]], axis=0).astype(BF16)
    low = lax.ppermute(last, "space", up)
    high = lax.ppermute(first, "space", down)

    pressure, source, concentration = (a.reshape(MODES, SLAB, CZ) for a in (pressure, source, concentration))
    mean_cond = mean_cond.reshape(SLAB, CZ)
    kl_cond = kl_cond.reshape(KL, SLAB, CZ)

    field = jax.ShapeDtypeStruct(pressure.shape, F32)
    plane = jax.ShapeDtypeStruct(mean_cond.shape, F32)
    dma = pltpu.SemaphoreType.DMA
    field_vmem = pltpu.VMEM(pressure.shape, F32)
    halo_vmem = pltpu.VMEM((2 * MODES, CY, CZ), BF16)
    edge_vmem = pltpu.VMEM((CY, CZ), F32)

    def rows_vmem(rows):
        return pltpu.VMEM((rows, CZ), F32)

    def message(rows):
        return jax.ShapeDtypeStruct((RANKS, rows, CZ), BF16)

    def message_vmem(rows):
        return pltpu.VMEM((RANKS, rows, CZ), BF16)

    def exchange(rows_of_ranks):
        return lax.all_to_all(rows_of_ranks, "mode", 0, 0, tiled=True)

    send, part = call(
        inner_kernel,
        (message(SENT), jax.ShapeDtypeStruct((4, SENT, CZ), F32)),
        [hbm()] * 2,
        [rows_vmem(2 * MODES * SPACED + 2 * PAD), rows_vmem(SLAB + PAD), rows_vmem(RANKS * STRIDE), message_vmem(SENT)]
        + [dma((2, MODES)), dma((RANKS,)), dma((4,))],
        "inner_images",
        size * 20,
        size * 14,
    )(pressure, concentration)
    send = call(
        outer_kernel,
        message(SENT),
        [hbm()] * 4,
        [
            rows_vmem(4 * STRIDE),
            halo_vmem,
            halo_vmem,
            rows_vmem(2 * CY),
            pltpu.VMEM((4, SENT, CZ), BF16),
            dma((6,)),
            dma((4,)),
        ],
        "outer_images",
        size,
        size,
        {3: 0},
    )(part, low, high, send)
    recv = exchange(send)

    own_rank = rank.reshape(1)
    head = call(
        head_kernel,
        plane,
        [smem(), smem()] + [hbm()] * 6,
        [rows_vmem(SLAB + 2 * PAD)] + [rows_vmem(SLAB)] * 3
        + [pltpu.VMEM((CY, CZ), BF16)] * 2 + [rows_vmem(SLAB)] * 2 + [dma((5,)), dma(()), dma(())],
        "head_part",
        size,
        size,
    )(own_rank, table, pressure, source, mean_cond, kl_cond, low, high)

    def partner(rows, bits):
        return lax.ppermute(rows, "mode", [(i, i ^ bits) for i in range(RANKS)])

    core = rank % 2
    half = SLAB // 2
    kept = lax.dynamic_slice_in_dim(head, core * half, half, 0)
    kept = kept + partner(lax.dynamic_slice_in_dim(head, (1 - core) * half, half, 0), 1)
    kept = (kept + partner(kept, 4)) + (partner(kept, 8) + partner(kept, 12))

    base_p, base_c = call(
        base_kernel,
        (field, field),
        [smem(), smem()] + [hbm()] * 6,
        [rows_vmem(2 * MODES * SPACED + 2 * PAD), field_vmem, rows_vmem(SLAB), halo_vmem, halo_vmem]
        + [field_vmem, field_vmem, rows_vmem(SLAB), dma((4 + 2 * MODES,)), dma((2,))],
        "base",
        size * 60,
        size * 24,
    )(own_rank, table, pressure, source, concentration, mean_cond, low, high)

    code = jnp.sum(table * POWERS.astype(np.int32)[:, None], axis=0)
    row = jnp.sum(jnp.where(code[None, :] == CODES[:, None], jnp.arange(ALL, dtype=jnp.int32)[None, :], 0), axis=1)
    places = row // MODES * STRIDE + row % MODES * SHARE

    own_kl = lax.dynamic_slice_in_dim(kl_cond, rank * SHARE, SHARE, 1)
    own_kl = jnp.pad(own_kl, ((0, 0), (0, FULL - SHARE), (0, 0)))

    recv, base_p, base_c, kept, places, own_kl = lax.optimization_barrier(
        (recv, base_p, base_c, kept, places, own_kl)
    )

    back = call(
        contract_kernel,
        message(SENT),
        [smem()] + [hbm()] * 2,
        [
            message_vmem(SENT),
            pltpu.VMEM((KL, FULL, CZ), F32),
            rows_vmem(RANKS * STRIDE),
            rows_vmem(VALID * FULL),
            pltpu.VMEM((ORDER * KL, FULL, CZ), F32),
            rows_vmem(RANKS * STRIDE),
            message_vmem(SENT),
            dma((RANKS,)),
            dma(()),
            dma((RANKS,)),
        ],
        "contract",
        size * 80,
        size * 16,
    )(places, recv, own_kl)
    kept = kept + partner(kept, 2)
    back, kept = lax.optimization_barrier((back, kept))
    received = exchange(back)

    other = partner(kept, 1)
    first_half = jnp.where(core == 0, kept, other)
    second_half = jnp.where(core == 0, other, kept)
    head = jnp.concatenate([first_half, second_half], axis=0)
    head_low = lax.ppermute(head[-CY:], "space", up)
    head_high = lax.ppermute(head[:CY], "space", down)
    moved = call(
        advection_kernel,
        field,
        [hbm()] * 8,
        [rows_vmem(MODES * SLAB + 2 * PAD), halo_vmem, halo_vmem, field_vmem, rows_vmem(SLAB)]
        + [rows_vmem(SLAB + 2 * PAD), edge_vmem, edge_vmem, field_vmem, pltpu.VMEM((3, SLAB, CZ), F32)]
        + [dma((7 + MODES,)), dma((MODES,))],
        "advection",
        size * 20,
        size * 12,
    )(concentration, low, high, base_c, mean_cond, head, head_low, head_high)
    pressure_next, concentration_next = call(
        result_kernel,
        (field, field),
        [hbm()] * 4,
        [message_vmem(SENT), rows_vmem(2 * MODES * SPACED), rows_vmem(SLAB), rows_vmem(SLAB + PAD)]
        + [rows_vmem(RANKS * STRIDE), rows_vmem(2 * MODES * SPACED)]
        + [dma((RANKS,)), dma((2, MODES)), dma(()), dma((2, MODES))],
        "result",
        size * 8,
        size * 20,
    )(received, base_p, moved, mean_cond)
    return (pressure_next.reshape(shape), concentration_next.reshape(shape))


def solution(mesh):
    return jax.shard_map(
        local,
        mesh=mesh,
        in_specs=(
            P("mode", "space", None, None),
            P("mode", "space", None, None),
            P("mode", "space", None, None),
            P("space", None, None),
            P(None, "space", None, None),
            P(),
        ),
        out_specs=(P("mode", "space", None, None), P("mode", "space", None, None)),
        check_vma=False,
    )
```

```python
import functools
import itertools

import jax
import jax.numpy as jnp
import numpy as np
from jax import lax
from jax.experimental import pallas as pl
from jax.experimental.pallas import tpu as pltpu
from jax.sharding import PartitionSpec as P

OMEGA = 0.8
DISPERSION = 0.01
STEP = 0.05
ORDER = 3

F32 = jnp.float32
BF16 = jnp.bfloat16

RANKS = 16
MODES = 11
PLANES = 11
CY = 32
CZ = 128
KL = 8
ALL = RANKS * MODES
SLAB = PLANES * CY
SHARE = SLAB // RANKS
FULL = 24
BODY = SHARE * MODES
PAD = 8
SPACED = SLAB + PAD

SENT = 496
STRIDE = SENT + PAD

EDGE_RANKS = (0, 1, RANKS - 2, RANKS - 1)
LIMIT = 63 * 1024 * 1024

INDICES = sorted(
    (t for t in itertools.product(range(ORDER + 1), repeat=KL) if sum(t) <= ORDER), key=lambda t: (sum(t), t)
)
PLACE = {t: i for i, t in enumerate(INDICES)}
NEIGHBOURS = [
    [
        (d, max(t[d], t[d] + step), PLACE[t[:d] + (t[d] + step,) + t[d + 1 :]])
        for d in range(KL)
        for step in (-1, 1)
        if t[:d] + (t[d] + step,) + t[d + 1 :] in PLACE
    ]
    for t in INDICES
]
VALID = len(INDICES)
POWERS = (ORDER + 1) ** np.arange(KL)
CODES = (np.array(INDICES) * POWERS).sum(axis=1).astype(np.int32)


def vmem():
    return pl.BlockSpec(memory_space=pltpu.VMEM)


def smem():
    return pl.BlockSpec(memory_space=pltpu.SMEM)


def hbm():
    return pl.BlockSpec(memory_space=pltpu.HBM)


def call(kernel, outs, ins, scratch, name, flops, moved, aliases=None):
    return pl.pallas_call(
        kernel,
        out_shape=outs,
        in_specs=ins,
        out_specs=jax.tree.map(lambda _: hbm(), outs),
        scratch_shapes=scratch,
        input_output_aliases=aliases or {},
        compiler_params=pltpu.CompilerParams(vmem_limit_bytes=LIMIT),
        cost_estimate=pl.CostEstimate(flops=flops, bytes_accessed=moved, transcendentals=0),
        name=name,
    )


def start_all(sems, pairs):
    copies = [pltpu.make_async_copy(source, target, sems.at[i]) for i, (source, target) in enumerate(pairs)]
    for copy in copies:
        copy.start()
    return copies


def loop(first, last, work):
    def one(i, carry):
        work(i)
        return carry

    lax.fori_loop(first, last, one, 0)


def edge_masks():
    row = lax.broadcasted_iota(jnp.int32, (CY, CZ), 0)
    lane = lax.broadcasted_iota(jnp.int32, (CY, CZ), 1)
    return row == 0, row == CY - 1, lane == 0, lane == CZ - 1


def rows_of(ref, start):
    return ref[pl.ds(start, CY), :]


def beside(ref, start, tile, masks):
    first_row, last_row, first_lane, last_lane = masks
    y_less = jnp.where(first_row, 0.0, rows_of(ref, start - 1))
    y_more = jnp.where(last_row, 0.0, rows_of(ref, start + 1))
    z_less = jnp.where(first_lane, 0.0, pltpu.roll(tile, 1, 1))
    z_more = jnp.where(last_lane, 0.0, pltpu.roll(tile, CZ - 1, 1))
    return y_less, y_more, z_less, z_more


def laplace(ref, base, x, masks, outer=None):
    start = base + x * CY
    tile = rows_of(ref, start)
    y_less, y_more, z_less, z_more = beside(ref, start, tile, masks)
    total = (y_more + y_less) + (z_more + z_less)
    if x > 0:
        total = total + rows_of(ref, start - CY)
    if x < PLANES - 1:
        total = total + rows_of(ref, start + CY)
    if outer is not None:
        total = total + outer
    return tile, 6.0 * tile - total


def rounded(tile):
    return tile.astype(BF16).astype(F32)


def copy_share(target, to, source, start):
    for part in range(0, FULL, 8):
        target[pl.ds(to + part, 8), :] = source[pl.ds(start + part, 8), :]


HALVES = ((0, BODY // 16), (BODY // 16, SENT // 16))


def half_rows(half):
    return pl.ds(half[0] * 16, (half[1] - half[0]) * 16)


def pack_rank(scratch, start, out_ref, slot, blocks):
    for block in blocks:
        out_ref[slot, pl.ds(block * 16, 16), :] = scratch[pl.ds(start + block * 16, 16), :].astype(BF16)


def unpack_rank(in_ref, rank, scratch, stride, blocks):
    for block in blocks:
        start = pl.multiple_of(rank * stride + block * 16, 8)
        scratch[pl.ds(start, 16), :] = in_ref[rank, pl.ds(block * 16, 16), :].astype(F32)


def inner_kernel(
    pressure_hbm, concentration_hbm, send_hbm, part_hbm, fields, image, scratch, strip, sems, send_sems, part_sems
):
    inputs = (pressure_hbm, concentration_hbm)

    def base_of(index, m):
        return pl.multiple_of(PAD + (index * MODES + m) * SPACED, 8)

    def fetch(index, m):
        target = fields.at[pl.ds(base_of(index, m), SLAB), :]
        return pltpu.make_async_copy(inputs[index].at[m], target, sems.at[index, m])

    for index in range(2):
        for m in range(MODES):
            fetch(index, m).start()
    for rank in range(RANKS):
        scratch[pl.ds(rank * STRIDE + 2 * BODY, SENT - 2 * BODY), :] = jnp.zeros((SENT - 2 * BODY, CZ), F32)
    masks = edge_masks()

    def send(index, rank):
        rows = half_rows(HALVES[index])
        return pltpu.make_async_copy(strip.at[rank, rows, :], send_hbm.at[rank, rows, :], send_sems.at[index, rank])

    for index in range(2):

        def one_mode(m):
            fetch(index, m).wait()
            for x in range(PLANES):
                image[pl.ds(x * CY, CY), :] = laplace(fields, base_of(index, m), x, masks)[1]
            for rank in range(RANKS):
                copy_share(scratch, rank * STRIDE + (index * MODES + m) * SHARE, image, rank * SHARE)

        loop(0, MODES, one_mode)

        def go(rank):
            pack_rank(scratch, pl.multiple_of(rank * STRIDE, 8), strip, rank, range(*HALVES[index]))
            send(index, rank).start()

        loop(2, RANKS - 2, go)
    parts = start_all(
        part_sems,
        [(scratch.at[pl.ds(rank * STRIDE, SENT), :], part_hbm.at[i]) for i, rank in enumerate(EDGE_RANKS)],
    )

    for copy in parts:
        copy.wait()
    for index in range(2):
        loop(2, RANKS - 2, lambda rank: send(index, rank).wait())


def outer_kernel(part_hbm, low_hbm, high_hbm, send_in, send_hbm, part, low, high, halo, strip, sems, send_sems):
    parts = [(part_hbm.at[i], part.at[pl.ds(i * STRIDE, SENT), :]) for i in range(4)]
    for copy in start_all(sems, parts + [(low_hbm, low), (high_hbm, high)]):
        copy.wait()

    def spread(mode):
        halo[pl.ds(0, CY), :] = low[mode].astype(F32)
        halo[pl.ds(CY, CY), :] = high[mode].astype(F32)
        row = mode * SHARE
        for i, at, of, count in (
            (0, 0, 0, SHARE),
            (1, 0, SHARE, CY - SHARE),
            (2, 2 * SHARE - CY, CY, CY - SHARE),
            (3, 0, 2 * CY - SHARE, SHARE),
        ):
            rows = pl.ds(i * STRIDE + row + at, count)
            part[rows, :] = part[rows, :] - halo[pl.ds(of, count), :]

    loop(0, 2 * MODES, spread)
    sends = []
    for i, rank in enumerate(EDGE_RANKS):
        pack_rank(part, i * STRIDE, strip, i, range(SENT // 16))
        send = pltpu.make_async_copy(strip.at[i], send_hbm.at[rank], send_sems.at[i])
        send.start()
        sends.append(send)
    for send in sends:
        send.wait()


def base_kernel(
    rank_ref, table_ref, pressure_hbm, source_hbm, concentration_hbm, mean_hbm, low_hbm, high_hbm,
    base_p_hbm, base_c_hbm,
    fields, source, mean, low, high, base_p, base_c, scale, sems, out_sems,
):
    copies = start_all(
        sems,
        [(mean_hbm, mean), (low_hbm, low), (high_hbm, high)]
        + [(pressure_hbm.at[m], fields.at[pl.ds(PAD + m * SPACED, SLAB), :]) for m in range(MODES)]
        + [(concentration_hbm.at[m], fields.at[pl.ds(PAD + (MODES + m) * SPACED, SLAB), :]) for m in range(MODES)]
        + [(source_hbm, source)],
    )
    for copy in copies:
        copy.wait()
    scale[...] = OMEGA / (6.0 * mean[...])
    masks = edge_masks()

    def one_mode(m):
        own = (table_ref[0, rank_ref[0] * MODES + m] >= 0).astype(F32)
        for index in range(2):
            base = pl.multiple_of(PAD + (index * MODES + m) * SPACED, 8)
            for x in range(PLANES):
                outer = None
                if x == 0:
                    outer = low[index * MODES + m].astype(F32)
                elif x == PLANES - 1:
                    outer = high[index * MODES + m].astype(F32)
                tile, image = laplace(fields, base, x, masks, outer)
                rows = pl.ds(x * CY, CY)
                term = own * (mean[rows, :] * rounded(image))
                if index == 0:
                    base_p[m, rows, :] = tile + scale[rows, :] * (source[m, rows, :] - term)
                else:
                    base_c[m, rows, :] = tile - DISPERSION * term

    loop(0, MODES, one_mode)
    for copy in start_all(out_sems, [(base_p, base_p_hbm), (base_c, base_c_hbm)]):
        copy.wait()


def head_kernel(
    rank_ref, table_ref, pressure_hbm, source_hbm, mean_hbm, kl_hbm, low_hbm, high_hbm, out_hbm,
    field, source, mean, kl, low, high, scale, out, sems, mean_sem, out_sem,
):
    fetch_mean = pltpu.make_async_copy(mean_hbm, mean, mean_sem)
    fetch_mean.start()
    out[...] = jnp.zeros((SLAB, CZ), F32)
    fetch_mean.wait()
    scale[...] = OMEGA / (6.0 * mean[...])
    masks = edge_masks()

    def one_mode(m):
        row = rank_ref[0] * MODES + m
        degree = table_ref[0, row]
        which = 0
        for d in range(1, KL):
            degree = degree + table_ref[d, row]
            which = which + d * table_ref[d, row]

        @pl.when((degree >= 0) & (degree <= 1))
        def _():
            copies = start_all(
                sems,
                [
                    (pressure_hbm.at[m], field.at[pl.ds(PAD, SLAB), :]),
                    (source_hbm.at[m], source),
                    (kl_hbm.at[which], kl),
                    (low_hbm.at[m], low),
                    (high_hbm.at[m], high),
                ],
            )
            for copy in copies:
                copy.wait()
            is_mean = (degree == 0).astype(F32)
            for x in range(PLANES):
                outer = None
                if x == 0:
                    outer = low[...].astype(F32)
                elif x == PLANES - 1:
                    outer = high[...].astype(F32)
                tile, image = laplace(field, PAD, x, masks, outer)
                image = rounded(image)
                rows = pl.ds(x * CY, CY)
                own = tile + scale[rows, :] * (source[rows, :] - mean[rows, :] * image)
                brought = scale[rows, :] * (kl[rows, :] * image)
                out[rows, :] = out[rows, :] + (is_mean * own - (1.0 - is_mean) * brought)

    loop(0, MODES, one_mode)
    leave = pltpu.make_async_copy(out, out_hbm, out_sem)
    leave.start()
    leave.wait()


def contract_kernel(
    places, recv_hbm, kl_hbm, send_hbm,
    recv, kl, images, ordered, weights, outs, strip, recv_sems, kl_sem, send_sems,
):
    def fetch(rank):
        return pltpu.make_async_copy(recv_hbm.at[rank], recv.at[rank], recv_sems.at[rank])

    loop(0, RANKS, lambda rank: fetch(rank).start())
    fetch_kl = pltpu.make_async_copy(kl_hbm, kl, kl_sem)
    fetch_kl.start()

    def clear(rank):
        outs[pl.ds(pl.multiple_of(rank * STRIDE, 8), SENT), :] = jnp.zeros((SENT, CZ), F32)

    loop(0, RANKS, clear)
    fetch_kl.wait()
    for larger in range(ORDER):
        root = float(np.sqrt(np.float32(larger + 1)).astype(jnp.bfloat16))
        for d in range(KL):
            weights[larger * KL + d] = root * kl[d]

    def spread(rank):
        fetch(rank).wait()
        unpack_rank(recv, rank, images, STRIDE, range(SENT // 16))

    loop(0, RANKS, spread)

    def send(index, rank):
        rows = half_rows(HALVES[index])
        return pltpu.make_async_copy(strip.at[rank, rows, :], send_hbm.at[rank, rows, :], send_sems.at[index, rank])

    def one_field(index):
        for i in range(VALID):
            copy_share(ordered, i * FULL, images, places[i] + index * BODY)
        for part in range(0, FULL, 8):
            count = min(8, SHARE - part)
            held = [weights[i, pl.ds(part, 8), :] for i in range(ORDER * KL)]
            for i in range(VALID):
                total = None
                for d, larger, other in NEIGHBOURS[i]:
                    term = held[(larger - 1) * KL + d] * ordered[pl.ds(other * FULL + part, 8), :]
                    total = term if total is None else total + term
                outs[pl.ds(places[i] + index * BODY + part, count), :] = total[:count]

        def go(rank):
            pack_rank(outs, pl.multiple_of(rank * STRIDE, 8), strip, rank, range(*HALVES[index]))
            send(index, rank).start()

        loop(0, RANKS, go)

    for index in range(2):
        one_field(index)
    for index in range(2):
        loop(0, RANKS, lambda rank: send(index, rank).wait())


def result_kernel(
    recv_hbm, base_p_hbm, base_c_hbm, mean_hbm, out_p_hbm, out_c_hbm,
    recv, base, mean, scale, sums, out, recv_sems, base_sems, mean_sem, sems,
):
    bases = (base_p_hbm, base_c_hbm)
    outputs = (out_p_hbm, out_c_hbm)

    def fetch(rank):
        return pltpu.make_async_copy(recv_hbm.at[rank], recv.at[rank], recv_sems.at[rank])

    def rows_at(index, m):
        return pl.ds(pl.multiple_of((index * MODES + m) * SPACED, 8), SLAB)

    def fetch_base(index, m):
        return pltpu.make_async_copy(bases[index].at[m], base.at[rows_at(index, m), :], base_sems.at[index, m])

    def leave(index, m):
        return pltpu.make_async_copy(out.at[rows_at(index, m), :], outputs[index].at[m], sems.at[index, m])

    loop(0, RANKS, lambda rank: fetch(rank).start())
    fetch_mean = pltpu.make_async_copy(mean_hbm, mean, mean_sem)
    fetch_mean.start()
    for index in range(2):
        loop(0, MODES, lambda m: fetch_base(index, m).start())
    fetch_mean.wait()
    scale[pl.ds(0, SLAB), :] = OMEGA / (6.0 * mean[...])

    def spread(rank):
        fetch(rank).wait()
        unpack_rank(recv, rank, sums, STRIDE, range(SENT // 16))

    loop(0, RANKS, spread)
    for index in range(2):

        def one_mode(m):
            fetch_base(index, m).wait()
            for rank in range(RANKS):
                for part in range(0, FULL, 8):
                    at = pl.ds((index * MODES + m) * SPACED + rank * SHARE + part, 8)
                    factor = DISPERSION if index else scale[pl.ds(rank * SHARE + part, 8), :]
                    total = sums[pl.ds(rank * STRIDE + (index * MODES + m) * SHARE + part, 8), :]
                    out[at, :] = base[at, :] - factor * total
            leave(index, m).start()

        loop(0, MODES, one_mode)
    for index in range(2):
        loop(0, MODES, lambda m: leave(index, m).wait())


def advection_kernel(
    field_hbm, low_hbm, high_hbm, base_hbm, mean_hbm, head_hbm, head_low_hbm, head_high_hbm, out_hbm,
    field, low, high, base, mean, head, head_low, head_high, out, speed, sems, out_sems,
):
    copies = start_all(
        sems,
        [
            (head_hbm, head.at[pl.ds(PAD, SLAB), :]),
            (head_low_hbm, head_low),
            (head_high_hbm, head_high),
            (mean_hbm, mean),
            (low_hbm, low),
            (high_hbm, high),
            (base_hbm, base),
        ]
        + [(field_hbm.at[m], field.at[pl.ds(PAD + m * SLAB, SLAB), :]) for m in range(MODES)],
    )
    masks = edge_masks()

    def steps(ref, base, x, outer):
        start = base + x * CY
        below = rows_of(ref, start - CY) if x > 0 else outer(0)
        above = rows_of(ref, start + CY) if x < PLANES - 1 else outer(1)
        y_less, y_more, z_less, z_more = beside(ref, start, rows_of(ref, start), masks)
        return above - below, y_more - y_less, z_more - z_less

    for copy in copies[:4]:
        copy.wait()
    for x in range(PLANES):
        rows = pl.ds(x * CY, CY)
        factor = (0.25 * STEP) * mean[rows, :]
        for axis, step in enumerate(steps(head, PAD, x, lambda side: (head_low, head_high)[side][...])):
            speed[axis, rows, :] = factor * step
    for copy in copies[4:]:
        copy.wait()

    def leave(m):
        return pltpu.make_async_copy(out.at[m], out_hbm.at[m], out_sems.at[m])

    def one_mode(m):
        for x in range(PLANES):
            rows = pl.ds(x * CY, CY)
            along = steps(
                field, pl.multiple_of(PAD + m * SLAB, 8), x, lambda side: (low, high)[side][MODES + m].astype(F32)
            )
            moved = sum(speed[axis, rows, :] * step for axis, step in enumerate(along))
            out[m, rows, :] = base[m, rows, :] + moved
        leave(m).start()

    loop(0, MODES, one_mode)
    loop(0, MODES, lambda m: leave(m).wait())


def local(pressure, source, concentration, mean_cond, kl_cond, mode_table):
    shape = pressure.shape
    spaces = lax.axis_size("space")
    up = [(i, i + 1) for i in range(spaces - 1)]
    down = [(i + 1, i) for i in range(spaces - 1)]
    rank = lax.axis_index("mode").astype(jnp.int32)
    table = mode_table.T
    size = pressure.size
    last = jnp.concatenate([pressure[:, -1], concentration[:, -1]], axis=0).astype(BF16)
    first = jnp.concatenate([pressure[:, 0], concentration[:, 0]], axis=0).astype(BF16)
    low = lax.ppermute(last, "space", up)
    high = lax.ppermute(first, "space", down)

    pressure, source, concentration = (a.reshape(MODES, SLAB, CZ) for a in (pressure, source, concentration))
    mean_cond = mean_cond.reshape(SLAB, CZ)
    kl_cond = kl_cond.reshape(KL, SLAB, CZ)

    field = jax.ShapeDtypeStruct(pressure.shape, F32)
    plane = jax.ShapeDtypeStruct(mean_cond.shape, F32)
    dma = pltpu.SemaphoreType.DMA
    field_vmem = pltpu.VMEM(pressure.shape, F32)
    halo_vmem = pltpu.VMEM((2 * MODES, CY, CZ), BF16)
    edge_vmem = pltpu.VMEM((CY, CZ), F32)

    def rows_vmem(rows):
        return pltpu.VMEM((rows, CZ), F32)

    def message(rows):
        return jax.ShapeDtypeStruct((RANKS, rows, CZ), BF16)

    def message_vmem(rows):
        return pltpu.VMEM((RANKS, rows, CZ), BF16)

    def exchange(rows_of_ranks):
        return lax.all_to_all(rows_of_ranks, "mode", 0, 0, tiled=True)

    send, part = call(
        inner_kernel,
        (message(SENT), jax.ShapeDtypeStruct((4, SENT, CZ), F32)),
        [hbm()] * 2,
        [rows_vmem(2 * MODES * SPACED + 2 * PAD), rows_vmem(SLAB + PAD), rows_vmem(RANKS * STRIDE), message_vmem(SENT)]
        + [dma((2, MODES)), dma((2, RANKS)), dma((4,))],
        "inner_images",
        size * 20,
        size * 14,
    )(pressure, concentration)
    send = call(
        outer_kernel,
        message(SENT),
        [hbm()] * 4,
        [
            rows_vmem(4 * STRIDE),
            halo_vmem,
            halo_vmem,
            rows_vmem(2 * CY),
            pltpu.VMEM((4, SENT, CZ), BF16),
            dma((6,)),
            dma((4,)),
        ],
        "outer_images",
        size,
        size,
        {3: 0},
    )(part, low, high, send)
    recv = exchange(send)

    own_rank = rank.reshape(1)
    head = call(
        head_kernel,
        plane,
        [smem(), smem()] + [hbm()] * 6,
        [rows_vmem(SLAB + 2 * PAD)] + [rows_vmem(SLAB)] * 3
        + [pltpu.VMEM((CY, CZ), BF16)] * 2 + [rows_vmem(SLAB)] * 2 + [dma((5,)), dma(()), dma(())],
        "head_part",
        size,
        size,
    )(own_rank, table, pressure, source, mean_cond, kl_cond, low, high)

    def partner(rows, bits):
        return lax.ppermute(rows, "mode", [(i, i ^ bits) for i in range(RANKS)])

    core = rank % 2
    half = SLAB // 2
    kept = lax.dynamic_slice_in_dim(head, core * half, half, 0)
    kept = kept + partner(lax.dynamic_slice_in_dim(head, (1 - core) * half, half, 0), 1)
    kept = (kept + partner(kept, 4)) + (partner(kept, 8) + partner(kept, 12))

    base_p, base_c = call(
        base_kernel,
        (field, field),
        [smem(), smem()] + [hbm()] * 6,
        [rows_vmem(2 * MODES * SPACED + 2 * PAD), field_vmem, rows_vmem(SLAB), halo_vmem, halo_vmem]
        + [field_vmem, field_vmem, rows_vmem(SLAB), dma((4 + 2 * MODES,)), dma((2,))],
        "base",
        size * 60,
        size * 24,
    )(own_rank, table, pressure, source, concentration, mean_cond, low, high)

    code = jnp.sum(table * POWERS.astype(np.int32)[:, None], axis=0)
    row = jnp.sum(jnp.where(code[None, :] == CODES[:, None], jnp.arange(ALL, dtype=jnp.int32)[None, :], 0), axis=1)
    places = row // MODES * STRIDE + row % MODES * SHARE

    own_kl = lax.dynamic_slice_in_dim(kl_cond, rank * SHARE, SHARE, 1)
    own_kl = jnp.pad(own_kl, ((0, 0), (0, FULL - SHARE), (0, 0)))

    recv, base_p, base_c, kept, places, own_kl = lax.optimization_barrier(
        (recv, base_p, base_c, kept, places, own_kl)
    )

    back = call(
        contract_kernel,
        message(SENT),
        [smem()] + [hbm()] * 2,
        [
            message_vmem(SENT),
            pltpu.VMEM((KL, FULL, CZ), F32),
            rows_vmem(RANKS * STRIDE),
            rows_vmem(VALID * FULL),
            pltpu.VMEM((ORDER * KL, FULL, CZ), F32),
            rows_vmem(RANKS * STRIDE),
            message_vmem(SENT),
            dma((RANKS,)),
            dma(()),
            dma((2, RANKS)),
        ],
        "contract",
        size * 80,
        size * 16,
    )(places, recv, own_kl)
    kept = kept + partner(kept, 2)
    back, kept = lax.optimization_barrier((back, kept))
    received = exchange(back)

    other = partner(kept, 1)
    first_half = jnp.where(core == 0, kept, other)
    second_half = jnp.where(core == 0, other, kept)
    head = jnp.concatenate([first_half, second_half], axis=0)
    head_low = lax.ppermute(head[-CY:], "space", up)
    head_high = lax.ppermute(head[:CY], "space", down)
    moved = call(
        advection_kernel,
        field,
        [hbm()] * 8,
        [rows_vmem(MODES * SLAB + 2 * PAD), halo_vmem, halo_vmem, field_vmem, rows_vmem(SLAB)]
        + [rows_vmem(SLAB + 2 * PAD), edge_vmem, edge_vmem, field_vmem, pltpu.VMEM((3, SLAB, CZ), F32)]
        + [dma((7 + MODES,)), dma((MODES,))],
        "advection",
        size * 20,
        size * 12,
    )(concentration, low, high, base_c, mean_cond, head, head_low, head_high)
    pressure_next, concentration_next = call(
        result_kernel,
        (field, field),
        [hbm()] * 4,
        [message_vmem(SENT), rows_vmem(2 * MODES * SPACED), rows_vmem(SLAB), rows_vmem(SLAB + PAD)]
        + [rows_vmem(RANKS * STRIDE), rows_vmem(2 * MODES * SPACED)]
        + [dma((RANKS,)), dma((2, MODES)), dma(()), dma((2, MODES))],
        "result",
        size * 8,
        size * 20,
    )(received, base_p, moved, mean_cond)
    return (pressure_next.reshape(shape), concentration_next.reshape(shape))


def solution(mesh):
    return jax.shard_map(
        local,
        mesh=mesh,
        in_specs=(
            P("mode", "space", None, None),
            P("mode", "space", None, None),
            P("mode", "space", None, None),
            P("space", None, None),
            P(None, "space", None, None),
            P(),
        ),
        out_specs=(P("mode", "space", None, None), P("mode", "space", None, None)),
        check_vma=False,
    )
```

```python
import functools
import itertools

import jax
import jax.numpy as jnp
import numpy as np
from jax import lax
from jax.experimental import pallas as pl
from jax.experimental.pallas import tpu as pltpu
from jax.sharding import PartitionSpec as P

OMEGA = 0.8
DISPERSION = 0.01
STEP = 0.05
ORDER = 3

F32 = jnp.float32
BF16 = jnp.bfloat16

RANKS = 16
MODES = 11
PLANES = 11
CY = 32
CZ = 128
KL = 8
ALL = RANKS * MODES
SLAB = PLANES * CY
SHARE = SLAB // RANKS
FULL = 24
BODY = SHARE * MODES
PAD = 8
SPACED = SLAB + PAD

SENT = 496
STRIDE = SENT + PAD

EDGE_RANKS = (0, 1, RANKS - 2, RANKS - 1)
LIMIT = 63 * 1024 * 1024

INDICES = sorted(
    (t for t in itertools.product(range(ORDER + 1), repeat=KL) if sum(t) <= ORDER), key=lambda t: (sum(t), t)
)
PLACE = {t: i for i, t in enumerate(INDICES)}
NEIGHBOURS = [
    [
        (d, max(t[d], t[d] + step), PLACE[t[:d] + (t[d] + step,) + t[d + 1 :]])
        for d in range(KL)
        for step in (-1, 1)
        if t[:d] + (t[d] + step,) + t[d + 1 :] in PLACE
    ]
    for t in INDICES
]
VALID = len(INDICES)
POWERS = (ORDER + 1) ** np.arange(KL)
CODES = (np.array(INDICES) * POWERS).sum(axis=1).astype(np.int32)


def vmem():
    return pl.BlockSpec(memory_space=pltpu.VMEM)


def smem():
    return pl.BlockSpec(memory_space=pltpu.SMEM)


def hbm():
    return pl.BlockSpec(memory_space=pltpu.HBM)


def call(kernel, outs, ins, scratch, name, flops, moved, aliases=None):
    return pl.pallas_call(
        kernel,
        out_shape=outs,
        in_specs=ins,
        out_specs=jax.tree.map(lambda _: hbm(), outs),
        scratch_shapes=scratch,
        input_output_aliases=aliases or {},
        compiler_params=pltpu.CompilerParams(vmem_limit_bytes=LIMIT),
        cost_estimate=pl.CostEstimate(flops=flops, bytes_accessed=moved, transcendentals=0),
        name=name,
    )


def start_all(sems, pairs):
    copies = [pltpu.make_async_copy(source, target, sems.at[i]) for i, (source, target) in enumerate(pairs)]
    for copy in copies:
        copy.start()
    return copies


def loop(first, last, work):
    def one(i, carry):
        work(i)
        return carry

    lax.fori_loop(first, last, one, 0)


def edge_masks():
    row = lax.broadcasted_iota(jnp.int32, (CY, CZ), 0)
    lane = lax.broadcasted_iota(jnp.int32, (CY, CZ), 1)
    return row == 0, row == CY - 1, lane == 0, lane == CZ - 1


def rows_of(ref, start):
    return ref[pl.ds(start, CY), :]


def beside(ref, start, tile, masks):
    first_row, last_row, first_lane, last_lane = masks
    y_less = jnp.where(first_row, 0.0, rows_of(ref, start - 1))
    y_more = jnp.where(last_row, 0.0, rows_of(ref, start + 1))
    z_less = jnp.where(first_lane, 0.0, pltpu.roll(tile, 1, 1))
    z_more = jnp.where(last_lane, 0.0, pltpu.roll(tile, CZ - 1, 1))
    return y_less, y_more, z_less, z_more


def laplace(ref, base, x, masks, outer=None):
    start = base + x * CY
    tile = rows_of(ref, start)
    y_less, y_more, z_less, z_more = beside(ref, start, tile, masks)
    total = (y_more + y_less) + (z_more + z_less)
    if x > 0:
        total = total + rows_of(ref, start - CY)
    if x < PLANES - 1:
        total = total + rows_of(ref, start + CY)
    if outer is not None:
        total = total + outer
    return tile, 6.0 * tile - total


def rounded(tile):
    return tile.astype(BF16).astype(F32)


def copy_share(target, to, source, start):
    for part in range(0, FULL, 8):
        target[pl.ds(to + part, 8), :] = source[pl.ds(start + part, 8), :]


HALVES = ((0, BODY // 16), (BODY // 16, SENT // 16))


def half_rows(half):
    return pl.ds(half[0] * 16, (half[1] - half[0]) * 16)


def pack_rank(scratch, start, out_ref, slot, blocks):
    for block in blocks:
        out_ref[slot, pl.ds(block * 16, 16), :] = scratch[pl.ds(start + block * 16, 16), :].astype(BF16)


def unpack_rank(in_ref, rank, scratch, stride, blocks):
    for block in blocks:
        start = pl.multiple_of(rank * stride + block * 16, 8)
        scratch[pl.ds(start, 16), :] = in_ref[rank, pl.ds(block * 16, 16), :].astype(F32)


def inner_kernel(
    pressure_hbm, concentration_hbm, send_hbm, part_hbm, fields, image, scratch, strip, sems, send_sems, part_sems
):
    inputs = (pressure_hbm, concentration_hbm)

    def base_of(index, m):
        return pl.multiple_of(PAD + (index * MODES + m) * SPACED, 8)

    def fetch(index, m):
        target = fields.at[pl.ds(base_of(index, m), SLAB), :]
        return pltpu.make_async_copy(inputs[index].at[m], target, sems.at[index, m])

    for index in range(2):
        for m in range(MODES):
            fetch(index, m).start()
    for rank in range(RANKS):
        scratch[pl.ds(rank * STRIDE + 2 * BODY, SENT - 2 * BODY), :] = jnp.zeros((SENT - 2 * BODY, CZ), F32)
    masks = edge_masks()

    def send(index, rank):
        rows = half_rows(HALVES[index])
        return pltpu.make_async_copy(strip.at[rank, rows, :], send_hbm.at[rank, rows, :], send_sems.at[index, rank])

    for index in range(2):

        def one_mode(m):
            fetch(index, m).wait()
            for x in range(PLANES):
                image[pl.ds(x * CY, CY), :] = laplace(fields, base_of(index, m), x, masks)[1]
            for rank in range(RANKS):
                copy_share(scratch, rank * STRIDE + (index * MODES + m) * SHARE, image, rank * SHARE)

        loop(0, MODES, one_mode)

        def go(rank):
            pack_rank(scratch, pl.multiple_of(rank * STRIDE, 8), strip, rank, range(*HALVES[index]))
            send(index, rank).start()

        loop(2, RANKS - 2, go)
    parts = start_all(
        part_sems,
        [(scratch.at[pl.ds(rank * STRIDE, SENT), :], part_hbm.at[i]) for i, rank in enumerate(EDGE_RANKS)],
    )

    for copy in parts:
        copy.wait()
    for index in range(2):
        loop(2, RANKS - 2, lambda rank: send(index, rank).wait())


def outer_kernel(part_hbm, low_hbm, high_hbm, send_in, send_hbm, part, low, high, halo, strip, sems, send_sems):
    parts = [(part_hbm.at[i], part.at[pl.ds(i * STRIDE, SENT), :]) for i in range(4)]
    for copy in start_all(sems, parts + [(low_hbm, low), (high_hbm, high)]):
        copy.wait()

    def spread(mode):
        halo[pl.ds(0, CY), :] = low[mode].astype(F32)
        halo[pl.ds(CY, CY), :] = high[mode].astype(F32)
        row = mode * SHARE
        for i, at, of, count in (
            (0, 0, 0, SHARE),
            (1, 0, SHARE, CY - SHARE),
            (2, 2 * SHARE - CY, CY, CY - SHARE),
            (3, 0, 2 * CY - SHARE, SHARE),
        ):
            rows = pl.ds(i * STRIDE + row + at, count)
            part[rows, :] = part[rows, :] - halo[pl.ds(of, count), :]

    loop(0, 2 * MODES, spread)
    sends = []
    for i, rank in enumerate(EDGE_RANKS):
        pack_rank(part, i * STRIDE, strip, i, range(SENT // 16))
        send = pltpu.make_async_copy(strip.at[i], send_hbm.at[rank], send_sems.at[i])
        send.start()
        sends.append(send)
    for send in sends:
        send.wait()


def base_kernel(
    rank_ref, table_ref, pressure_hbm, source_hbm, concentration_hbm, mean_hbm, low_hbm, high_hbm,
    base_p_hbm, base_c_hbm,
    fields, source, mean, low, high, base_p, base_c, scale, sems, out_sems,
):
    copies = start_all(
        sems,
        [(mean_hbm, mean), (low_hbm, low), (high_hbm, high)]
        + [(pressure_hbm.at[m], fields.at[pl.ds(PAD + m * SPACED, SLAB), :]) for m in range(MODES)]
        + [(concentration_hbm.at[m], fields.at[pl.ds(PAD + (MODES + m) * SPACED, SLAB), :]) for m in range(MODES)]
        + [(source_hbm, source)],
    )
    for copy in copies:
        copy.wait()
    scale[...] = OMEGA / (6.0 * mean[...])
    masks = edge_masks()

    def one_mode(m):
        own = (table_ref[0, rank_ref[0] * MODES + m] >= 0).astype(F32)
        for index in range(2):
            base = pl.multiple_of(PAD + (index * MODES + m) * SPACED, 8)
            for x in range(PLANES):
                outer = None
                if x == 0:
                    outer = low[index * MODES + m].astype(F32)
                elif x == PLANES - 1:
                    outer = high[index * MODES + m].astype(F32)
                tile, image = laplace(fields, base, x, masks, outer)
                rows = pl.ds(x * CY, CY)
                term = own * (mean[rows, :] * rounded(image))
                if index == 0:
                    base_p[m, rows, :] = tile + scale[rows, :] * (source[m, rows, :] - term)
                else:
                    base_c[m, rows, :] = tile - DISPERSION * term

    loop(0, MODES, one_mode)
    for copy in start_all(out_sems, [(base_p, base_p_hbm), (base_c, base_c_hbm)]):
        copy.wait()


def head_kernel(
    rank_ref, table_ref, pressure_hbm, source_hbm, mean_hbm, kl_hbm, low_hbm, high_hbm, out_hbm,
    field, source, mean, kl, low, high, scale, out, sems, mean_sem, out_sem,
):
    fetch_mean = pltpu.make_async_copy(mean_hbm, mean, mean_sem)
    fetch_mean.start()
    out[...] = jnp.zeros((SLAB, CZ), F32)
    fetch_mean.wait()
    scale[...] = OMEGA / (6.0 * mean[...])
    masks = edge_masks()

    def one_mode(m):
        row = rank_ref[0] * MODES + m
        degree = table_ref[0, row]
        which = 0
        for d in range(1, KL):
            degree = degree + table_ref[d, row]
            which = which + d * table_ref[d, row]

        @pl.when((degree >= 0) & (degree <= 1))
        def _():
            copies = start_all(
                sems,
                [
                    (pressure_hbm.at[m], field.at[pl.ds(PAD, SLAB), :]),
                    (source_hbm.at[m], source),
                    (kl_hbm.at[which], kl),
                    (low_hbm.at[m], low),
                    (high_hbm.at[m], high),
                ],
            )
            for copy in copies:
                copy.wait()
            is_mean = (degree == 0).astype(F32)
            for x in range(PLANES):
                outer = None
                if x == 0:
                    outer = low[...].astype(F32)
                elif x == PLANES - 1:
                    outer = high[...].astype(F32)
                tile, image = laplace(field, PAD, x, masks, outer)
                image = rounded(image)
                rows = pl.ds(x * CY, CY)
                own = tile + scale[rows, :] * (source[rows, :] - mean[rows, :] * image)
                brought = scale[rows, :] * (kl[rows, :] * image)
                out[rows, :] = out[rows, :] + (is_mean * own - (1.0 - is_mean) * brought)

    loop(0, MODES, one_mode)
    leave = pltpu.make_async_copy(out, out_hbm, out_sem)
    leave.start()
    leave.wait()


def contract_kernel(
    places, recv_hbm, kl_hbm, send_hbm,
    recv, kl, images, ordered, weights, outs, strip, recv_sems, kl_sem, send_sems,
):
    def fetch(rank):
        return pltpu.make_async_copy(recv_hbm.at[rank], recv.at[rank], recv_sems.at[rank])

    loop(0, RANKS, lambda rank: fetch(rank).start())
    fetch_kl = pltpu.make_async_copy(kl_hbm, kl, kl_sem)
    fetch_kl.start()

    def clear(rank):
        outs[pl.ds(pl.multiple_of(rank * STRIDE, 8), SENT), :] = jnp.zeros((SENT, CZ), F32)

    loop(0, RANKS, clear)
    fetch_kl.wait()
    for larger in range(ORDER):
        root = float(np.sqrt(np.float32(larger + 1)).astype(jnp.bfloat16))
        for d in range(KL):
            weights[larger * KL + d] = root * kl[d]

    def spread(rank):
        fetch(rank).wait()
        unpack_rank(recv, rank, images, STRIDE, range(SENT // 16))

    loop(0, RANKS, spread)

    def send(index, rank):
        rows = half_rows(HALVES[index])
        return pltpu.make_async_copy(strip.at[rank, rows, :], send_hbm.at[rank, rows, :], send_sems.at[index, rank])

    def one_field(index):
        for i in range(VALID):
            copy_share(ordered, i * FULL, images, places[i] + index * BODY)
        for part in range(0, FULL, 8):
            count = min(8, SHARE - part)
            held = [weights[i, pl.ds(part, 8), :] for i in range(ORDER * KL)]
            for i in range(VALID):
                total = None
                for d, larger, other in NEIGHBOURS[i]:
                    term = held[(larger - 1) * KL + d] * ordered[pl.ds(other * FULL + part, 8), :]
                    total = term if total is None else total + term
                outs[pl.ds(places[i] + index * BODY + part, count), :] = total[:count]

        def go(rank):
            pack_rank(outs, pl.multiple_of(rank * STRIDE, 8), strip, rank, range(*HALVES[index]))
            send(index, rank).start()

        loop(0, RANKS, go)

    for index in range(2):
        one_field(index)
    for index in range(2):
        loop(0, RANKS, lambda rank: send(index, rank).wait())


def result_kernel(
    recv_hbm, base_p_hbm, base_c_hbm, mean_hbm, out_p_hbm, out_c_hbm,
    recv, base, mean, scale, sums, out, recv_sems, base_sems, mean_sem, sems,
):
    bases = (base_p_hbm, base_c_hbm)
    outputs = (out_p_hbm, out_c_hbm)

    def fetch(rank):
        return pltpu.make_async_copy(recv_hbm.at[rank], recv.at[rank], recv_sems.at[rank])

    def rows_at(index, m):
        return pl.ds(pl.multiple_of((index * MODES + m) * SPACED, 8), SLAB)

    def fetch_base(index, m):
        return pltpu.make_async_copy(bases[index].at[m], base.at[rows_at(index, m), :], base_sems.at[index, m])

    def leave(index, m):
        return pltpu.make_async_copy(out.at[rows_at(index, m), :], outputs[index].at[m], sems.at[index, m])

    loop(0, RANKS, lambda rank: fetch(rank).start())
    fetch_mean = pltpu.make_async_copy(mean_hbm, mean, mean_sem)
    fetch_mean.start()
    for index in range(2):
        loop(0, MODES, lambda m: fetch_base(index, m).start())
    fetch_mean.wait()
    scale[pl.ds(0, SLAB), :] = OMEGA / (6.0 * mean[...])

    loop(0, RANKS, lambda rank: fetch(rank).wait())
    whole = (BODY + 15) // 16
    for index, blocks in enumerate((range(whole), range(whole, SENT // 16))):

        def spread(rank):
            unpack_rank(recv, rank, sums, STRIDE, blocks)

        def one_mode(m):
            fetch_base(index, m).wait()
            for rank in range(RANKS):
                for part in range(0, FULL, 8):
                    at = pl.ds((index * MODES + m) * SPACED + rank * SHARE + part, 8)
                    factor = DISPERSION if index else scale[pl.ds(rank * SHARE + part, 8), :]
                    total = sums[pl.ds(rank * STRIDE + (index * MODES + m) * SHARE + part, 8), :]
                    out[at, :] = base[at, :] - factor * total
            leave(index, m).start()

        loop(0, RANKS, spread)
        loop(0, MODES, one_mode)
    for index in range(2):
        loop(0, MODES, lambda m: leave(index, m).wait())


def advection_kernel(
    field_hbm, low_hbm, high_hbm, base_hbm, mean_hbm, head_hbm, head_low_hbm, head_high_hbm, out_hbm,
    field, low, high, base, mean, head, head_low, head_high, out, speed, sems, out_sems,
):
    copies = start_all(
        sems,
        [
            (head_hbm, head.at[pl.ds(PAD, SLAB), :]),
            (head_low_hbm, head_low),
            (head_high_hbm, head_high),
            (mean_hbm, mean),
            (low_hbm, low),
            (high_hbm, high),
            (base_hbm, base),
        ]
        + [(field_hbm.at[m], field.at[pl.ds(PAD + m * SLAB, SLAB), :]) for m in range(MODES)],
    )
    masks = edge_masks()

    def steps(ref, base, x, outer):
        start = base + x * CY
        below = rows_of(ref, start - CY) if x > 0 else outer(0)
        above = rows_of(ref, start + CY) if x < PLANES - 1 else outer(1)
        y_less, y_more, z_less, z_more = beside(ref, start, rows_of(ref, start), masks)
        return above - below, y_more - y_less, z_more - z_less

    for copy in copies[:4]:
        copy.wait()
    for x in range(PLANES):
        rows = pl.ds(x * CY, CY)
        factor = (0.25 * STEP) * mean[rows, :]
        for axis, step in enumerate(steps(head, PAD, x, lambda side: (head_low, head_high)[side][...])):
            speed[axis, rows, :] = factor * step
    for copy in copies[4:]:
        copy.wait()

    def leave(m):
        return pltpu.make_async_copy(out.at[m], out_hbm.at[m], out_sems.at[m])

    def one_mode(m):
        for x in range(PLANES):
            rows = pl.ds(x * CY, CY)
            along = steps(
                field, pl.multiple_of(PAD + m * SLAB, 8), x, lambda side: (low, high)[side][MODES + m].astype(F32)
            )
            moved = sum(speed[axis, rows, :] * step for axis, step in enumerate(along))
            out[m, rows, :] = base[m, rows, :] + moved
        leave(m).start()

    loop(0, MODES, one_mode)
    loop(0, MODES, lambda m: leave(m).wait())


def local(pressure, source, concentration, mean_cond, kl_cond, mode_table):
    shape = pressure.shape
    spaces = lax.axis_size("space")
    up = [(i, i + 1) for i in range(spaces - 1)]
    down = [(i + 1, i) for i in range(spaces - 1)]
    rank = lax.axis_index("mode").astype(jnp.int32)
    table = mode_table.T
    size = pressure.size
    last = jnp.concatenate([pressure[:, -1], concentration[:, -1]], axis=0).astype(BF16)
    first = jnp.concatenate([pressure[:, 0], concentration[:, 0]], axis=0).astype(BF16)
    low = lax.ppermute(last, "space", up)
    high = lax.ppermute(first, "space", down)

    pressure, source, concentration = (a.reshape(MODES, SLAB, CZ) for a in (pressure, source, concentration))
    mean_cond = mean_cond.reshape(SLAB, CZ)
    kl_cond = kl_cond.reshape(KL, SLAB, CZ)

    field = jax.ShapeDtypeStruct(pressure.shape, F32)
    plane = jax.ShapeDtypeStruct(mean_cond.shape, F32)
    dma = pltpu.SemaphoreType.DMA
    field_vmem = pltpu.VMEM(pressure.shape, F32)
    halo_vmem = pltpu.VMEM((2 * MODES, CY, CZ), BF16)
    edge_vmem = pltpu.VMEM((CY, CZ), F32)

    def rows_vmem(rows):
        return pltpu.VMEM((rows, CZ), F32)

    def message(rows):
        return jax.ShapeDtypeStruct((RANKS, rows, CZ), BF16)

    def message_vmem(rows):
        return pltpu.VMEM((RANKS, rows, CZ), BF16)

    def exchange(rows_of_ranks):
        return lax.all_to_all(rows_of_ranks, "mode", 0, 0, tiled=True)

    send, part = call(
        inner_kernel,
        (message(SENT), jax.ShapeDtypeStruct((4, SENT, CZ), F32)),
        [hbm()] * 2,
        [rows_vmem(2 * MODES * SPACED + 2 * PAD), rows_vmem(SLAB + PAD), rows_vmem(RANKS * STRIDE), message_vmem(SENT)]
        + [dma((2, MODES)), dma((2, RANKS)), dma((4,))],
        "inner_images",
        size * 20,
        size * 14,
    )(pressure, concentration)
    send = call(
        outer_kernel,
        message(SENT),
        [hbm()] * 4,
        [
            rows_vmem(4 * STRIDE),
            halo_vmem,
            halo_vmem,
            rows_vmem(2 * CY),
            pltpu.VMEM((4, SENT, CZ), BF16),
            dma((6,)),
            dma((4,)),
        ],
        "outer_images",
        size,
        size,
        {3: 0},
    )(part, low, high, send)
    recv = exchange(send)

    own_rank = rank.reshape(1)
    head = call(
        head_kernel,
        plane,
        [smem(), smem()] + [hbm()] * 6,
        [rows_vmem(SLAB + 2 * PAD)] + [rows_vmem(SLAB)] * 3
        + [pltpu.VMEM((CY, CZ), BF16)] * 2 + [rows_vmem(SLAB)] * 2 + [dma((5,)), dma(()), dma(())],
        "head_part",
        size,
        size,
    )(own_rank, table, pressure, source, mean_cond, kl_cond, low, high)

    def partner(rows, bits):
        return lax.ppermute(rows, "mode", [(i, i ^ bits) for i in range(RANKS)])

    core = rank % 2
    half = SLAB // 2
    kept = lax.dynamic_slice_in_dim(head, core * half, half, 0)
    kept = kept + partner(lax.dynamic_slice_in_dim(head, (1 - core) * half, half, 0), 1)
    kept = (kept + partner(kept, 4)) + (partner(kept, 8) + partner(kept, 12))

    base_p, base_c = call(
        base_kernel,
        (field, field),
        [smem(), smem()] + [hbm()] * 6,
        [rows_vmem(2 * MODES * SPACED + 2 * PAD), field_vmem, rows_vmem(SLAB), halo_vmem, halo_vmem]
        + [field_vmem, field_vmem, rows_vmem(SLAB), dma((4 + 2 * MODES,)), dma((2,))],
        "base",
        size * 60,
        size * 24,
    )(own_rank, table, pressure, source, concentration, mean_cond, low, high)

    code = jnp.sum(table * POWERS.astype(np.int32)[:, None], axis=0)
    row = jnp.sum(jnp.where(code[None, :] == CODES[:, None], jnp.arange(ALL, dtype=jnp.int32)[None, :], 0), axis=1)
    places = row // MODES * STRIDE + row % MODES * SHARE

    own_kl = lax.dynamic_slice_in_dim(kl_cond, rank * SHARE, SHARE, 1)
    own_kl = jnp.pad(own_kl, ((0, 0), (0, FULL - SHARE), (0, 0)))

    recv, base_p, base_c, kept, places, own_kl = lax.optimization_barrier(
        (recv, base_p, base_c, kept, places, own_kl)
    )

    back = call(
        contract_kernel,
        message(SENT),
        [smem()] + [hbm()] * 2,
        [
            message_vmem(SENT),
            pltpu.VMEM((KL, FULL, CZ), F32),
            rows_vmem(RANKS * STRIDE),
            rows_vmem(VALID * FULL),
            pltpu.VMEM((ORDER * KL, FULL, CZ), F32),
            rows_vmem(RANKS * STRIDE),
            message_vmem(SENT),
            dma((RANKS,)),
            dma(()),
            dma((2, RANKS)),
        ],
        "contract",
        size * 80,
        size * 16,
    )(places, recv, own_kl)
    kept = kept + partner(kept, 2)
    back, kept = lax.optimization_barrier((back, kept))
    received = exchange(back)

    other = partner(kept, 1)
    first_half = jnp.where(core == 0, kept, other)
    second_half = jnp.where(core == 0, other, kept)
    head = jnp.concatenate([first_half, second_half], axis=0)
    head_low = lax.ppermute(head[-CY:], "space", up)
    head_high = lax.ppermute(head[:CY], "space", down)
    moved = call(
        advection_kernel,
        field,
        [hbm()] * 8,
        [rows_vmem(MODES * SLAB + 2 * PAD), halo_vmem, halo_vmem, field_vmem, rows_vmem(SLAB)]
        + [rows_vmem(SLAB + 2 * PAD), edge_vmem, edge_vmem, field_vmem, pltpu.VMEM((3, SLAB, CZ), F32)]
        + [dma((7 + MODES,)), dma((MODES,))],
        "advection",
        size * 20,
        size * 12,
    )(concentration, low, high, base_c, mean_cond, head, head_low, head_high)
    pressure_next, concentration_next = call(
        result_kernel,
        (field, field),
        [hbm()] * 4,
        [message_vmem(SENT), rows_vmem(2 * MODES * SPACED), rows_vmem(SLAB), rows_vmem(SLAB + PAD)]
        + [rows_vmem(RANKS * STRIDE), rows_vmem(2 * MODES * SPACED)]
        + [dma((RANKS,)), dma((2, MODES)), dma(()), dma((2, MODES))],
        "result",
        size * 8,
        size * 20,
    )(received, base_p, moved, mean_cond)
    return (pressure_next.reshape(shape), concentration_next.reshape(shape))


def solution(mesh):
    return jax.shard_map(
        local,
        mesh=mesh,
        in_specs=(
            P("mode", "space", None, None),
            P("mode", "space", None, None),
            P("mode", "space", None, None),
            P("space", None, None),
            P(None, "space", None, None),
            P(),
        ),
        out_specs=(P("mode", "space", None, None), P("mode", "space", None, None)),
        check_vma=False,
    )
```
